256 devices in a mesh: segment: 4 (over y_hi, core), frame: 64 (over x, z, y_lo).
Axes of the slice: x: 4, y: 4 (y_hi: 2, y_lo: 2; y = y_hi * 2 + y_lo), z: 8, core: 2. Of those that a mesh axis runs over, the one named last changes fastest.
Arguments:
- clips: bfloat16 [4, 64, 320, 1024], P('segment', 'frame'), may hold values from -6 to 6
- timesteps: int32 [4], replicated, may hold values from 0 to 999
- gain: float32 [4, 320], replicated, may hold values from 0.25 to 1.75
- temporal_weight: bfloat16 [4, 3, 320, 320], P('segment'), may hold values from -0.1875 to 0.1875
- film_weight: bfloat16 [4, 320, 320], P('segment'), may hold values from -0.3125 to 0.3125
- out_weight: bfloat16 [4, 320, 320], P('segment'), may hold values from -0.3125 to 0.3125
- skip_weight: bfloat16 [2, 320, 320], replicated, may hold values from -0.3125 to 0.3125
Outputs:
- video_out: bfloat16 [4, 64, 320, 1024], P('segment', 'frame')
The draws below stay inside these ranges and needn't reach their ends.
All inputs are finite; a program needn't handle non-finite values.
Results may differ from the reference program's by a relative error of at most 0.012.
Values may be sent and summed in bfloat16 or wider, within the bound.
A program may use at most 64 MiB of HBM per device.

```python
import math
import jax
import jax.numpy as jnp
from jax import lax

C = 320
PIX = 1024
MB = 4
FRAMES = 64


def with_ends(drawn, key, low, high):
    extent = drawn.shape
    place = [jax.random.randint(jax.random.fold_in(key, axis), (), 0, extent[axis]) for axis in range(len(extent))]
    drawn = drawn.at[tuple(place)].set(low)
    longest = extent.index(max(extent))
    place[longest] = (place[longest] + 1) % extent[longest]
    return drawn.at[tuple(place)].set(high)


def shard_levels(own_key, shape, cuts, low, high):
    loudness = 1.0
    for dim, shards_of in cuts:
        steps = jax.random.uniform(jax.random.fold_in(jax.random.fold_in(own_key, 6), dim), (shards_of,), jnp.float32, low / len(cuts), high / len(cuts))
        loudness = loudness * jnp.repeat(jnp.exp(steps), shape[dim] // shards_of).reshape((-1,) + (1,) * (len(shape) - 1 - dim))
    return loudness


def centred(stream_key, shape, deviation, bound, cuts=(), held_as=jnp.bfloat16):
    result = jax.random.normal(stream_key, shape, jnp.float32) * deviation
    if len(cuts) > 0:
        result = shard_levels(stream_key, shape, cuts, -0.22, 0.18) * result
    return jnp.clip(result, min=-bound, max=bound).astype(held_as)


def setup_inputs(seed: int = 0) -> dict:
    arg_keys = jax.random.split(jax.random.key(seed), 8)
    clips = centred(arg_keys[0], (MB, FRAMES, C, PIX), 1.0, 6.0, ((0, 4), (1, 64)))
    timesteps = with_ends(jax.random.randint(arg_keys[1], (MB,), 0, 1000), jax.random.fold_in(arg_keys[1], 1), 0, 999).astype(jnp.int32)
    gain = jnp.clip(1.0 + 0.15 * jax.random.normal(arg_keys[2], (MB, C), jnp.float32), 0.25, 1.75)
    temporal_weight = centred(arg_keys[3], (MB, 3, C, C), (3 * C) ** -0.5, 0.1875, ((0, 4),))
    film_weight = centred(arg_keys[4], (MB, C, C), C ** -0.5, 0.3125, ((0, 4),))
    out_weight = centred(arg_keys[5], (MB, C, C), C ** -0.5, 0.3125, ((0, 4),))
    skip_weight = centred(arg_keys[6], (2, C, C), C ** -0.5, 0.3125)
    return {"clips": clips, "timesteps": timesteps, "gain": gain, "temporal_weight": temporal_weight, "film_weight": film_weight, "out_weight": out_weight, "skip_weight": skip_weight}


def embed(timesteps, width):
    half = width // 2
    freq = jnp.exp(-math.log(10000.0) * jnp.arange(half, dtype=jnp.float32) / half)
    angle = timesteps.astype(jnp.float32)[:, None] * freq[None, :]
    return jnp.concatenate([jnp.sin(angle), jnp.cos(angle)], axis=-1).astype(jnp.bfloat16)

def reference(clips, timesteps, gain, temporal_weight, film_weight, out_weight, skip_weight):
    emb = embed(timesteps, C)
    frames = clips.shape[1]
    outputs = []
    state = clips
    for section in range(4):
        film = jnp.dot(emb, film_weight[section], preferred_element_type=jnp.float32)
        values = state.astype(jnp.float32)
        meansq = lax.optimization_barrier(jnp.mean(values * values, axis=2, keepdims=True))
        normed = (values * jax.lax.rsqrt(meansq + 1e-05) * gain[section][None, None, :, None]).astype(jnp.bfloat16)
        padded = jnp.pad(normed, ((0, 0), (1, 1), (0, 0), (0, 0))).astype(jnp.float32)
        mixed = jnp.zeros(values.shape, jnp.float32)
        for tap in range(3):
            mixed = mixed + jnp.einsum('io,mfip->mfop', temporal_weight[section, tap].astype(jnp.float32), padded[:, tap:tap + frames])
        hidden = jax.nn.silu(mixed * (1.0 + film[:, None, :, None])).astype(jnp.bfloat16)
        total = values + jnp.einsum('io,mfip->mfop', out_weight[section].astype(jnp.float32), hidden.astype(jnp.float32))
        if section == 2:
            total = total + jnp.einsum('io,mfip->mfop', skip_weight[0].astype(jnp.float32), outputs[0].astype(jnp.float32))
        if section == 3:
            total = total + jnp.einsum('io,mfip->mfop', skip_weight[1].astype(jnp.float32), clips.astype(jnp.float32))
        state = total.astype(jnp.bfloat16)
        outputs.append(state)
    return state
```

```python
import functools
import math

import jax
import jax.numpy as jnp
import numpy as np
from jax import lax
from jax.experimental import pallas as pl
from jax.experimental.pallas import tpu as pltpu
from jax.sharding import PartitionSpec as P

MESH = pl.DeviceIdType.MESH
LANES = 128
SECTIONS = 4
EMB_ROWS = 16


def unet_kernel(
    geometry,
    time_ref,
    freq_ref,
    gain_ref,
    taps_ref,
    film_ref,
    proj_ref,
    skip_ref,
    clips_ref,
    out_ref,
    raw,
    raw_skip,
    raw_film,
    wt,
    skt,
    film_rows,
    film_col,
    gain_col,
    state,
    nrm,
    halo_l,
    halo_r,
    load_sem,
    take_sem,
    swap_send,
    swap_recv,
    halo_send,
    halo_recv,
    own_send,
    own_recv,
    cut_send,
    cut_recv,
    side_send,
    side_recv,
    sib_send,
    sib_recv,
    film_send,
    film_recv,
    back_take,
    back_send,
    back_recv,
):
    C, chunks, frames, x_step, pieces = geometry
    half = pieces // 2
    rows = C // pieces
    half_pix = chunks * LANES
    groups = frames // 2
    f32, bf16 = jnp.float32, jnp.bfloat16

    seg = lax.axis_index("segment")
    frame = lax.axis_index("frame")
    y_hi, core = seg // 2, seg % 2
    group, y_lo = frame // 2, frame % 2
    x_par = (frame // x_step) % 2

    partner = (seg, group * 2 + 1 - y_lo)
    left = (seg, frame - 2)
    right = (seg, frame + 2)
    sibling = (y_hi * 2 + 1 - core, frame)
    across = ((1 - y_hi) * 2 + core, group * 2 + 1 - y_lo)
    beside = (seg, frame + x_step - 2 * x_step * x_par)
    has_left = group > 0
    has_right = group < groups - 1
    gathered = (1 - y_hi) * 2 + core
    relayed = (1 - y_hi) * 2 + 1 - core
    sib_own = y_hi * 2 + 1 - core

    def remote(src, dst, send, recv, device):
        return pltpu.make_async_remote_copy(
            src_ref=src, dst_ref=dst, send_sem=send, recv_sem=recv, device_id=device, device_id_type=MESH
        )

    loads = [
        pltpu.make_async_copy(taps_ref.at[0, 0], raw.at[pl.ds(0, C)], load_sem.at[0]),
        pltpu.make_async_copy(taps_ref.at[0, 1], raw.at[pl.ds(C, C)], load_sem.at[1]),
        pltpu.make_async_copy(taps_ref.at[0, 2], raw.at[pl.ds(2 * C, C)], load_sem.at[2]),
        pltpu.make_async_copy(proj_ref.at[0], raw.at[pl.ds(3 * C, C)], load_sem.at[3]),
        pltpu.make_async_copy(film_ref.at[0], raw_film, load_sem.at[4]),
        pltpu.make_async_copy(skip_ref.at[0], raw_skip.at[pl.ds(0, C)], load_sem.at[5]),
        pltpu.make_async_copy(skip_ref.at[1], raw_skip.at[pl.ds(C, C)], load_sem.at[6]),
    ]
    for load in loads:
        load.start()

    barrier = pltpu.get_barrier_semaphore()
    for device in (partner, sibling, across, beside):
        pl.semaphore_signal(barrier, inc=1, device_id=device, device_id_type=MESH)

    @pl.when(has_left)
    def _():
        pl.semaphore_signal(barrier, inc=1, device_id=left, device_id_type=MESH)

    @pl.when(has_right)
    def _():
        pl.semaphore_signal(barrier, inc=1, device_id=right, device_id_type=MESH)

    pl.semaphore_wait(barrier, 4 + has_left.astype(jnp.int32) + has_right.astype(jnp.int32))

    def pixels(part, c):
        return pl.ds(pl.multiple_of(part * half_pix + c * LANES, LANES), LANES)

    def swap(c):
        return remote(
            clips_ref.at[0, 0, :, pixels(1 - y_lo, c)],
            state.at[0, y_lo, c],
            swap_send.at[c],
            swap_recv.at[c],
            partner,
        )

    def take(c):
        return pltpu.make_async_copy(
            clips_ref.at[0, 0, :, pixels(y_lo, c)], state.at[0, y_lo, c], take_sem.at[c]
        )

    for c in range(chunks):
        swap(c).start()
        take(c).start()

    for load in loads[:4]:
        load.wait()
    for k in range(4 * C // LANES):
        wt[seg, :, k * LANES : (k + 1) * LANES] = raw[k * LANES : (k + 1) * LANES, :].T

    def own_piece(i):
        q = pl.ds(pl.multiple_of((x_par * half + i) * rows, 16), rows)
        return q

    to_sibling = remote(wt.at[seg], wt.at[seg], own_send.at[0], own_recv.at[0], sibling)
    from_sibling = remote(wt.at[sib_own], wt.at[sib_own], own_send.at[0], own_recv.at[0], sibling)
    to_sibling.start()

    def cut_out(i):
        q = own_piece(i)
        return remote(wt.at[seg, q], wt.at[seg, q], cut_send.at[i], cut_recv.at[i], across)

    def cut_in(i):
        q = own_piece(i)
        return remote(wt.at[gathered, q], wt.at[gathered, q], cut_send.at[i], cut_recv.at[i], across)

    def side_out(i):
        q = own_piece(i)
        return remote(wt.at[gathered, q], wt.at[gathered, q], side_send.at[i], side_recv.at[i], beside)

    def side_rows(i):
        return pl.ds(pl.multiple_of(((1 - x_par) * half + i) * rows, 16), rows)

    def side_in(i):
        q = side_rows(i)
        return remote(wt.at[gathered, q], wt.at[gathered, q], side_send.at[i], side_recv.at[i], beside)

    def sib_out(kind, i):
        q = own_piece(i) if kind == 0 else side_rows(i)
        return remote(wt.at[gathered, q], wt.at[gathered, q], sib_send.at[kind, i], sib_recv.at[kind, i], sibling)

    def sib_in(kind, i):
        q = own_piece(i) if kind == 0 else side_rows(i)
        return remote(wt.at[relayed, q], wt.at[relayed, q], sib_send.at[kind, i], sib_recv.at[kind, i], sibling)

    def forward(i):
        cut_in(i).wait_recv()
        side_out(i).start()
        sib_out(0, i).start()
        side_in(i).wait_recv()
        sib_out(1, i).start()

    def from_relay():
        for kind in range(2):
            for i in range(half):
                sib_in(kind, i).wait_recv()

    @pl.when(core == 0)
    def _():
        for i in range(half):
            cut_out(i).start()

    row = lax.broadcasted_iota(jnp.int32, (EMB_ROWS, 1), 0)
    when = jnp.zeros((EMB_ROWS, 1), jnp.int32)
    for m in range(SECTIONS):
        when = jnp.where(row == m, time_ref[m], when)
    angle = when.astype(f32) * freq_ref[...]
    lane = lax.broadcasted_iota(jnp.int32, angle.shape, 1)
    emb = jnp.where(lane < C // 2, jnp.sin(angle), jnp.cos(angle)).astype(bf16)
    loads[4].wait()
    film_rows[seg] = jnp.dot(emb, raw_film[...], preferred_element_type=f32)

    def film_copy(index, which, device):
        return remote(film_rows.at[index], film_rows.at[index], film_send.at[which], film_recv.at[which], device)

    film_copy(seg, 0, sibling).start()
    film_copy(seg, 1, across).start()

    def column(values):
        return jnp.broadcast_to(values, (LANES, C)).T

    for s in range(SECTIONS):
        gain_col[s] = column(gain_ref[s : s + 1, :])

    @pl.when(jnp.logical_not(has_left))
    def _():
        halo_l[...] = jnp.zeros_like(halo_l)

    @pl.when(jnp.logical_not(has_right))
    def _():
        halo_r[...] = jnp.zeros_like(halo_r)

    def to_left(s, c):
        return remote(nrm.at[s, 0, c], halo_r.at[s, c], halo_send.at[0, s, c], halo_recv.at[1, s, c], left)

    def to_right(s, c):
        return remote(nrm.at[s, 1, c], halo_l.at[s, c], halo_send.at[1, s, c], halo_recv.at[0, s, c], right)

    def normalize(values, s, c):
        meansq = jnp.sum(values * values, axis=0, keepdims=True) * (1.0 / C)
        scale = lax.rsqrt(meansq + 1e-05)
        gain = gain_col[s]
        nrm[s, 0, c] = (values[:, :LANES] * scale[:, :LANES] * gain).astype(bf16)
        nrm[s, 1, c] = (values[:, LANES:] * scale[:, LANES:] * gain).astype(bf16)

        @pl.when(has_left)
        def _():
            to_left(s, c).start()

        @pl.when(has_right)
        def _():
            to_right(s, c).start()

    def both(s, c):
        return jnp.concatenate([state[s, 0, c], state[s, 1, c]], axis=1)

    def first(c, carry):
        take(c).wait()
        swap_in = remote(
            clips_ref.at[0, 0, :, pixels(y_lo, c)],
            state.at[0, 1 - y_lo, c],
            swap_send.at[c],
            swap_recv.at[c],
            partner,
        )
        swap_in.wait_recv()
        normalize(both(0, c).astype(f32), 0, c)
        return carry

    lax.fori_loop(0, chunks, first, 0)

    @pl.when(core == 1)
    def _():
        for i in range(half):
            cut_out(i).start()

    for load in loads[5:]:
        load.wait()
    for n in range(2):
        for k in range(C // LANES + 1):
            lo, hi = k * LANES, min((k + 1) * LANES, C)
            skt[n, :, lo:hi] = raw_skip[n * C + lo : n * C + hi, :].T

    early = jnp.logical_and(y_hi == 1, core == 0)

    def pass_film():
        film_copy(gathered, 1, across).wait_recv()
        film_copy(gathered, 2, sibling).start()

    @pl.when(early)
    def _():
        pass_film()
        for i in range(half):
            forward(i)

    def back_own(c):
        return pltpu.make_async_copy(
            state.at[SECTIONS, y_lo, c], out_ref.at[0, 0, :, pixels(y_lo, c)], back_take.at[c]
        )

    def back_out(c):
        return remote(
            state.at[SECTIONS, 1 - y_lo, c],
            out_ref.at[0, 0, :, pixels(y_lo, c)],
            back_send.at[c],
            back_recv.at[c],
            partner,
        )

    def back_in(c):
        return remote(
            state.at[SECTIONS, 1 - y_lo, c],
            out_ref.at[0, 0, :, pixels(1 - y_lo, c)],
            back_send.at[c],
            back_recv.at[c],
            partner,
        )

    for s in range(SECTIONS):
        @pl.when(sib_own == s)
        def _():
            from_sibling.wait_recv()
            film_copy(sib_own, 0, sibling).wait_recv()

        @pl.when(relayed == s)
        def _():
            from_relay()
            film_copy(relayed, 2, sibling).wait_recv()

        mine = jnp.sum(jnp.where(row == seg, film_rows[s], 0.0), axis=0, keepdims=True)
        film_col[...] = column(1.0 + mine)

        def step(c, carry):
            @pl.when(has_left)
            def _():
                to_right(s, c).wait_recv()

            @pl.when(has_right)
            def _():
                to_left(s, c).wait_recv()

            n0, n1 = nrm[s, 0, c], nrm[s, 1, c]
            pad = jnp.zeros((4 * C - 3 * C - 2 * LANES, 2 * LANES), bf16)
            window = jnp.concatenate(
                [
                    jnp.concatenate([halo_l[s, c], n0], axis=1),
                    jnp.concatenate([n0, n1], axis=1),
                    jnp.concatenate([n1, halo_r[s, c]], axis=1),
                    pad,
                ],
                axis=0,
            )
            mixed = jnp.dot(wt[s, :, : 8 * LANES], window, preferred_element_type=f32)
            scale = film_col[...]
            hidden = jax.nn.silu(mixed * jnp.concatenate([scale, scale], axis=1)).astype(bf16)
            weights = wt[s, :, 7 * LANES :]
            fields = jnp.concatenate([pad, hidden], axis=0)
            if s == 2:
                weights = jnp.concatenate([weights, skt[0]], axis=1)
                fields = jnp.concatenate([fields, both(1, c)], axis=0)
            if s == 3:
                weights = jnp.concatenate([weights, skt[1]], axis=1)
                fields = jnp.concatenate([fields, both(0, c)], axis=0)
            total = both(s, c).astype(f32) + jnp.dot(weights, fields, preferred_element_type=f32)
            result = total.astype(bf16)
            state[s + 1, 0, c] = result[:, :LANES]
            state[s + 1, 1, c] = result[:, LANES:]
            if s + 1 < SECTIONS:
                normalize(result.astype(f32), s + 1, c)
            else:
                back_own(c).start()
                back_out(c).start()
            if s == 0:

                @pl.when(jnp.logical_not(early))
                def _():
                    forward(c)

            return carry

        lax.fori_loop(0, chunks, step, 0)
        if s == 0:

            @pl.when(jnp.logical_not(early))
            def _():
                for i in range(chunks, half):
                    forward(i)
                pass_film()

    def finish(c, carry):
        swap(c).wait_send()
        back_own(c).wait()
        back_out(c).wait_send()
        back_in(c).wait_recv()
        return carry

    lax.fori_loop(0, chunks, finish, 0)

    def sent(t, carry):
        s, c = t // chunks, t % chunks

        @pl.when(has_left)
        def _():
            to_left(s, c).wait_send()

        @pl.when(has_right)
        def _():
            to_right(s, c).wait_send()

        return carry

    lax.fori_loop(0, SECTIONS * chunks, sent, 0)
    to_sibling.wait_send()
    for i in range(half):
        cut_out(i).wait_send()
        side_out(i).wait_send()
        sib_out(0, i).wait_send()
        sib_out(1, i).wait_send()
    film_copy(seg, 0, sibling).wait_send()
    film_copy(seg, 1, across).wait_send()
    film_copy(gathered, 2, sibling).wait_send()


def shards(geometry, clips, timesteps, gain, temporal_weight, film_weight, out_weight, skip_weight):
    C, chunks, frames, x_step, pieces = geometry
    half = pieces // 2
    base = np.exp(-math.log(10000.0) * np.arange(C // 2) / (C // 2))
    freq = jnp.asarray(np.concatenate([base, base])[None, :].astype(np.float32))
    vmem = pl.BlockSpec(memory_space=pltpu.VMEM)
    any_space = pl.BlockSpec(memory_space=pl.ANY)
    bf16, f32 = jnp.bfloat16, jnp.float32
    dma = pltpu.SemaphoreType.DMA
    flops = 2 * 18 * C * C * 2 * chunks * LANES
    return pl.pallas_call(
        functools.partial(unet_kernel, geometry),
        out_shape=jax.ShapeDtypeStruct(clips.shape, bf16),
        in_specs=[
            pl.BlockSpec(memory_space=pltpu.SMEM),
            vmem,
            vmem,
            any_space,
            any_space,
            any_space,
            any_space,
            any_space,
        ],
        out_specs=any_space,
        scratch_shapes=[
            pltpu.VMEM((4 * C, C), bf16),
            pltpu.VMEM((2 * C, C), bf16),
            pltpu.VMEM((C, C), bf16),
            pltpu.VMEM((SECTIONS, C, 4 * C), bf16),
            pltpu.VMEM((2, C, C), bf16),
            pltpu.VMEM((SECTIONS, EMB_ROWS, C), f32),
            pltpu.VMEM((C, LANES), f32),
            pltpu.VMEM((SECTIONS, C, LANES), f32),
            pltpu.VMEM((SECTIONS + 1, 2, chunks, C, LANES), bf16),
            pltpu.VMEM((SECTIONS, 2, chunks, C, LANES), bf16),
            pltpu.VMEM((SECTIONS, chunks, C, LANES), bf16),
            pltpu.VMEM((SECTIONS, chunks, C, LANES), bf16),
            dma((7,)),
            dma((chunks,)),
            dma((chunks,)),
            dma((chunks,)),
            dma((2, SECTIONS, chunks)),
            dma((2, SECTIONS, chunks)),
            dma((1,)),
            dma((1,)),
            dma((half,)),
            dma((half,)),
            dma((half,)),
            dma((half,)),
            dma((2, half)),
            dma((2, half)),
            dma((3,)),
            dma((3,)),
            dma((chunks,)),
            dma((chunks,)),
            dma((chunks,)),
        ],
        compiler_params=pltpu.CompilerParams(
            collective_id=0, has_side_effects=True, vmem_limit_bytes=48 * 2**20
        ),
        cost_estimate=pl.CostEstimate(flops=flops, bytes_accessed=4 * clips.size, transcendentals=0),
        name="unet",
    )(timesteps, freq, gain, temporal_weight, film_weight, out_weight, skip_weight, clips)


def solution(mesh):
    frames = mesh.shape["frame"]

    def run(clips, *rest):
        _, _, C, pix = clips.shape
        x_step = 16 if frames >= 32 else 2
        geometry = (C, pix // 2 // LANES, frames, x_step, C // 32)
        return shards(geometry, clips, *rest)

    placed = (
        P("segment", "frame", None, None),
        P(),
        P(),
        P("segment", None, None, None),
        P("segment", None, None),
        P("segment", None, None),
        P(),
    )
    return jax.shard_map(
        run,
        mesh=mesh,
        in_specs=placed,
        out_specs=P("segment", "frame", None, None),
        check_vma=False,
    )
```

```python
import functools
import math

import jax
import jax.numpy as jnp
import numpy as np
from jax import lax
from jax.experimental import pallas as pl
from jax.experimental.pallas import tpu as pltpu
from jax.sharding import PartitionSpec as P

MESH = pl.DeviceIdType.MESH
LANES = 128
SECTIONS = 4
EMB_ROWS = 8


def unet_kernel(
    geometry,
    time_ref,
    freq_ref,
    gain_ref,
    taps_ref,
    film_ref,
    proj_ref,
    skip_ref,
    clips_ref,
    out_ref,
    time_smem,
    freq_vmem,
    gain_vmem,
    raw,
    raw_skip,
    raw_film,
    wt,
    skt,
    film_rows,
    film_col,
    gain_col,
    state,
    nrm,
    halo_l,
    halo_r,
    load_sem,
    take_sem,
    swap_send,
    swap_recv,
    halo_send,
    halo_recv,
    own_send,
    own_recv,
    cut_send,
    cut_recv,
    side_send,
    side_recv,
    sib_send,
    sib_recv,
    film_send,
    film_recv,
    back_take,
    back_send,
    back_recv,
):
    C, chunks, frames = geometry
    pieces = 4 * C // LANES
    half = pieces // 2
    half_pix = chunks * LANES
    groups = frames // 2
    f32, bf16 = jnp.float32, jnp.bfloat16

    seg = lax.axis_index("segment")
    frame = lax.axis_index("frame")
    y_hi, core = seg // 2, seg % 2
    group, y_lo = frame // 2, frame % 2

    partner = (seg, group * 2 + 1 - y_lo)
    left = (seg, frame - 2)
    right = (seg, frame + 2)
    sibling = (y_hi * 2 + 1 - core, frame)
    across = ((1 - y_hi) * 2 + core, group * 2 + 1 - y_lo)
    has_left = group > 0
    has_right = group < groups - 1
    gathered = (1 - y_hi) * 2 + core
    relayed = (1 - y_hi) * 2 + 1 - core
    sib_own = y_hi * 2 + 1 - core

    def remote(src, dst, send, recv, device):
        return pltpu.make_async_remote_copy(
            src_ref=src, dst_ref=dst, send_sem=send, recv_sem=recv, device_id=device, device_id_type=MESH
        )

    loads = [
        pltpu.make_async_copy(taps_ref.at[0, 0], raw.at[pl.ds(0, C)], load_sem.at[0]),
        pltpu.make_async_copy(taps_ref.at[0, 1], raw.at[pl.ds(C, C)], load_sem.at[1]),
        pltpu.make_async_copy(taps_ref.at[0, 2], raw.at[pl.ds(2 * C, C)], load_sem.at[2]),
        pltpu.make_async_copy(proj_ref.at[0], raw.at[pl.ds(3 * C, C)], load_sem.at[3]),
        pltpu.make_async_copy(film_ref.at[0], raw_film, load_sem.at[4]),
        pltpu.make_async_copy(skip_ref.at[0], raw_skip.at[pl.ds(0, C)], load_sem.at[5]),
        pltpu.make_async_copy(skip_ref.at[1], raw_skip.at[pl.ds(C, C)], load_sem.at[6]),
        pltpu.make_async_copy(time_ref, time_smem, load_sem.at[7]),
        pltpu.make_async_copy(freq_ref, freq_vmem, load_sem.at[8]),
        pltpu.make_async_copy(gain_ref, gain_vmem, load_sem.at[9]),
    ]
    for load in loads:
        load.start()

    def pixels(part, c):
        return pl.ds(pl.multiple_of(part * half_pix + c * LANES, LANES), LANES)

    def take(c):
        return pltpu.make_async_copy(
            clips_ref.at[0, 0, :, pixels(y_lo, c)], state.at[0, y_lo, c], take_sem.at[c]
        )

    for c in range(chunks):
        take(c).start()

    barrier = pltpu.get_barrier_semaphore()
    for device in (partner, sibling, across):
        pl.semaphore_signal(barrier, inc=1, device_id=device, device_id_type=MESH)

    @pl.when(has_left)
    def _():
        pl.semaphore_signal(barrier, inc=1, device_id=left, device_id_type=MESH)

    @pl.when(has_right)
    def _():
        pl.semaphore_signal(barrier, inc=1, device_id=right, device_id_type=MESH)

    for load in loads[:4]:
        load.wait()
    for k in range(pieces):
        wt[seg, :, k * LANES : (k + 1) * LANES] = raw[k * LANES : (k + 1) * LANES, :].T

    pl.semaphore_wait(barrier, 3 + has_left.astype(jnp.int32) + has_right.astype(jnp.int32))

    def swap(c):
        return remote(
            clips_ref.at[0, 0, :, pixels(1 - y_lo, c)],
            state.at[0, y_lo, c],
            swap_send.at[c],
            swap_recv.at[c],
            partner,
        )

    for c in range(chunks):
        swap(c).start()

    early = jnp.logical_and(y_hi == 1, core == 0)
    first_source = jnp.logical_and(y_hi == 0, core == 0)

    def block(index, q):
        return wt.at[index, :, pl.ds(pl.multiple_of(q * LANES, LANES), LANES)]

    def own_to_sibling(index):
        return remote(wt.at[index], wt.at[index], own_send.at[0], own_recv.at[0], sibling)

    def to_across(index, q):
        return remote(block(index, q), block(index, q), cut_send.at[q], cut_recv.at[q], across)

    def to_partner(index, q):
        return remote(block(index, q), block(index, q), side_send.at[q], side_recv.at[q], partner)

    def to_sibling(index, q):
        return remote(block(index, q), block(index, q), sib_send.at[q], sib_recv.at[q], sibling)

    def forward_all(q):
        to_across(gathered, q).wait_recv()
        to_sibling(gathered, q).start()

    def forward_cut(i):
        q = 2 * i + y_lo
        to_across(gathered, q).wait_recv()
        to_partner(gathered, q).start()
        to_sibling(gathered, q).start()

    def forward_side(i):
        q = 2 * i + 1 - y_lo
        to_partner(gathered, q).wait_recv()
        to_sibling(gathered, q).start()

    @pl.when(first_source)
    def _():
        for q in range(pieces):
            to_across(seg, q).start()

    own_to_sibling(seg).start()

    for load in loads[7:]:
        load.wait()
    row = lax.broadcasted_iota(jnp.int32, (EMB_ROWS, 1), 0)
    when = jnp.zeros((EMB_ROWS, 1), jnp.int32)
    for m in range(SECTIONS):
        when = jnp.where(row == m, time_smem[m], when)
    angle = when.astype(f32) * freq_vmem[...]
    lane = lax.broadcasted_iota(jnp.int32, angle.shape, 1)
    emb = jnp.where(lane < C // 2, jnp.sin(angle), jnp.cos(angle)).astype(bf16)
    loads[4].wait()
    film_rows[seg] = jnp.dot(emb, raw_film[...], preferred_element_type=f32)

    def film_copy(index, which, device):
        return remote(film_rows.at[index], film_rows.at[index], film_send.at[which], film_recv.at[which], device)

    film_copy(seg, 0, sibling).start()
    film_copy(seg, 1, across).start()

    def column(values):
        return jnp.broadcast_to(values, (LANES, C)).T

    for s in range(SECTIONS):
        gain_col[s] = column(gain_vmem[s : s + 1, :])

    @pl.when(jnp.logical_not(has_left))
    def _():
        halo_l[...] = jnp.zeros_like(halo_l)

    @pl.when(jnp.logical_not(has_right))
    def _():
        halo_r[...] = jnp.zeros_like(halo_r)

    def to_left(s, c):
        return remote(nrm.at[s, 0, c], halo_r.at[s, c], halo_send.at[0, s, c], halo_recv.at[1, s, c], left)

    def to_right(s, c):
        return remote(nrm.at[s, 1, c], halo_l.at[s, c], halo_send.at[1, s, c], halo_recv.at[0, s, c], right)

    def normalize(values, s, c):
        meansq = jnp.sum(values * values, axis=0, keepdims=True) * (1.0 / C)
        scale = lax.rsqrt(meansq + 1e-05)
        gain = gain_col[s]
        nrm[s, 0, c] = (values[:, :LANES] * scale[:, :LANES] * gain).astype(bf16)
        nrm[s, 1, c] = (values[:, LANES:] * scale[:, LANES:] * gain).astype(bf16)

        @pl.when(has_left)
        def _():
            to_left(s, c).start()

        @pl.when(has_right)
        def _():
            to_right(s, c).start()

    def both(s, c):
        return jnp.concatenate([state[s, 0, c], state[s, 1, c]], axis=1)

    def first(c, carry):
        take(c).wait()
        swap_in = remote(
            clips_ref.at[0, 0, :, pixels(y_lo, c)],
            state.at[0, 1 - y_lo, c],
            swap_send.at[c],
            swap_recv.at[c],
            partner,
        )
        swap_in.wait_recv()
        normalize(both(0, c).astype(f32), 0, c)

        @pl.when(early)
        def _():
            forward_all(2 * c)
            forward_all(2 * c + 1)

        return carry

    for load in loads[5:7]:
        load.wait()
    for n in range(2):
        for k in range(C // LANES + 1):
            lo, hi = k * LANES, min((k + 1) * LANES, C)
            skt[n, :, lo:hi] = raw_skip[n * C + lo : n * C + hi, :].T

    lax.fori_loop(0, chunks, first, 0)

    @pl.when(jnp.logical_not(first_source))
    def _():
        for i in range(half):
            to_across(seg, 2 * i + 1 - y_lo).start()

    def pass_film():
        film_copy(gathered, 1, across).wait_recv()
        film_copy(gathered, 2, sibling).start()

    @pl.when(early)
    def _():
        for q in range(min(2 * chunks, pieces), pieces):
            forward_all(q)
        pass_film()

    def back_own(c):
        return pltpu.make_async_copy(
            state.at[SECTIONS, y_lo, c], out_ref.at[0, 0, :, pixels(y_lo, c)], back_take.at[c]
        )

    def back_out(c):
        return remote(
            state.at[SECTIONS, 1 - y_lo, c],
            out_ref.at[0, 0, :, pixels(y_lo, c)],
            back_send.at[c],
            back_recv.at[c],
            partner,
        )

    def back_in(c):
        return remote(
            state.at[SECTIONS, 1 - y_lo, c],
            out_ref.at[0, 0, :, pixels(1 - y_lo, c)],
            back_send.at[c],
            back_recv.at[c],
            partner,
        )

    for s in range(SECTIONS):
        @pl.when(sib_own == s)
        def _():
            own_to_sibling(sib_own).wait_recv()
            film_copy(sib_own, 0, sibling).wait_recv()

        @pl.when(relayed == s)
        def _():
            for q in range(pieces):
                to_sibling(relayed, q).wait_recv()
            film_copy(relayed, 2, sibling).wait_recv()

        mine = jnp.sum(jnp.where(row == seg, film_rows[s], 0.0), axis=0, keepdims=True)
        film_col[...] = column(1.0 + mine)

        def step(c, carry):
            @pl.when(has_left)
            def _():
                to_right(s, c).wait_recv()

            @pl.when(has_right)
            def _():
                to_left(s, c).wait_recv()

            n0, n1 = nrm[s, 0, c], nrm[s, 1, c]
            pad = jnp.zeros((4 * C - 3 * C - 2 * LANES, 2 * LANES), bf16)
            window = jnp.concatenate(
                [
                    jnp.concatenate([halo_l[s, c], n0], axis=1),
                    jnp.concatenate([n0, n1], axis=1),
                    jnp.concatenate([n1, halo_r[s, c]], axis=1),
                    pad,
                ],
                axis=0,
            )
            mixed = jnp.dot(wt[s, :, : 8 * LANES], window, preferred_element_type=f32)
            scale = film_col[...]
            hidden = jax.nn.silu(mixed * jnp.concatenate([scale, scale], axis=1)).astype(bf16)
            weights = wt[s, :, 7 * LANES :]
            fields = jnp.concatenate([pad, hidden], axis=0)
            if s == 2:
                weights = jnp.concatenate([weights, skt[0]], axis=1)
                fields = jnp.concatenate([fields, both(1, c)], axis=0)
            if s == 3:
                weights = jnp.concatenate([weights, skt[1]], axis=1)
                fields = jnp.concatenate([fields, both(0, c)], axis=0)
            total = both(s, c).astype(f32) + jnp.dot(weights, fields, preferred_element_type=f32)
            result = total.astype(bf16)
            state[s + 1, 0, c] = result[:, :LANES]
            state[s + 1, 1, c] = result[:, LANES:]
            if s + 1 < SECTIONS:
                normalize(result.astype(f32), s + 1, c)
            else:
                back_own(c).start()
                back_out(c).start()
            if s == 0:

                @pl.when(jnp.logical_not(early))
                def _():
                    forward_cut(c)

                    @pl.when(c >= 2)
                    def _():
                        forward_side(c - 2)

            return carry

        lax.fori_loop(0, chunks, step, 0)
        if s == 0:

            @pl.when(jnp.logical_not(early))
            def _():
                for i in range(chunks, half):
                    forward_cut(i)
                for i in range(max(chunks - 2, 0), half):
                    forward_side(i)
                pass_film()

    def finish(c, carry):
        swap(c).wait_send()
        back_own(c).wait()
        back_out(c).wait_send()
        back_in(c).wait_recv()
        return carry

    lax.fori_loop(0, chunks, finish, 0)

    def sent(t, carry):
        s, c = t // chunks, t % chunks

        @pl.when(has_left)
        def _():
            to_left(s, c).wait_send()

        @pl.when(has_right)
        def _():
            to_right(s, c).wait_send()

        return carry

    lax.fori_loop(0, SECTIONS * chunks, sent, 0)
    own_to_sibling(seg).wait_send()

    @pl.when(first_source)
    def _():
        for q in range(pieces):
            to_across(seg, q).wait_send()

    @pl.when(jnp.logical_not(first_source))
    def _():
        for i in range(half):
            to_across(seg, 2 * i + 1 - y_lo).wait_send()

    @pl.when(jnp.logical_not(early))
    def _():
        for i in range(half):
            to_partner(gathered, 2 * i + y_lo).wait_send()

    for q in range(pieces):
        to_sibling(gathered, q).wait_send()
    film_copy(seg, 0, sibling).wait_send()
    film_copy(seg, 1, across).wait_send()
    film_copy(gathered, 2, sibling).wait_send()


def shards(geometry, clips, timesteps, gain, temporal_weight, film_weight, out_weight, skip_weight):
    C, chunks, frames = geometry
    pieces = 4 * C // LANES
    base = np.exp(-math.log(10000.0) * np.arange(C // 2) / (C // 2))
    freq = jnp.asarray(np.concatenate([base, base])[None, :].astype(np.float32))
    hbm = pl.BlockSpec(memory_space=pltpu.HBM)
    bf16, f32 = jnp.bfloat16, jnp.float32
    dma = pltpu.SemaphoreType.DMA
    flops = 2 * 18 * C * C * 2 * chunks * LANES
    return pl.pallas_call(
        functools.partial(unet_kernel, geometry),
        out_shape=jax.ShapeDtypeStruct(clips.shape, bf16),
        in_specs=[hbm] * 8,
        out_specs=hbm,
        scratch_shapes=[
            pltpu.SMEM(timesteps.shape, jnp.int32),
            pltpu.VMEM(freq.shape, f32),
            pltpu.VMEM(gain.shape, f32),
            pltpu.VMEM((4 * C, C), bf16),
            pltpu.VMEM((2 * C, C), bf16),
            pltpu.VMEM((C, C), bf16),
            pltpu.VMEM((SECTIONS, C, 4 * C), bf16),
            pltpu.VMEM((2, C, C), bf16),
            pltpu.VMEM((SECTIONS, EMB_ROWS, C), f32),
            pltpu.VMEM((C, LANES), f32),
            pltpu.VMEM((SECTIONS, C, LANES), f32),
            pltpu.VMEM((SECTIONS + 1, 2, chunks, C, LANES), bf16),
            pltpu.VMEM((SECTIONS, 2, chunks, C, LANES), bf16),
            pltpu.VMEM((SECTIONS, chunks, C, LANES), bf16),
            pltpu.VMEM((SECTIONS, chunks, C, LANES), bf16),
            dma((10,)),
            dma((chunks,)),
            dma((chunks,)),
            dma((chunks,)),
            dma((2, SECTIONS, chunks)),
            dma((2, SECTIONS, chunks)),
            dma((1,)),
            dma((1,)),
            dma((pieces,)),
            dma((pieces,)),
            dma((pieces,)),
            dma((pieces,)),
            dma((pieces,)),
            dma((pieces,)),
            dma((3,)),
            dma((3,)),
            dma((chunks,)),
            dma((chunks,)),
            dma((chunks,)),
        ],
        compiler_params=pltpu.CompilerParams(
            collective_id=0, has_side_effects=True, vmem_limit_bytes=63 * 2**20
        ),
        cost_estimate=pl.CostEstimate(flops=flops, bytes_accessed=4 * clips.size, transcendentals=0),
        name="unet",
    )(timesteps, freq, gain, temporal_weight, film_weight, out_weight, skip_weight, clips)


def solution(mesh):
    frames = mesh.shape["frame"]

    def run(clips, *rest):
        _, _, C, pix = clips.shape
        geometry = (C, pix // 2 // LANES, frames)
        return shards(geometry, clips, *rest)

    placed = (
        P("segment", "frame", None, None),
        P(),
        P(),
        P("segment", None, None, None),
        P("segment", None, None),
        P("segment", None, None),
        P(),
    )
    return jax.shard_map(
        run,
        mesh=mesh,
        in_specs=placed,
        out_specs=P("segment", "frame", None, None),
        check_vma=False,
    )
```

```python
import functools
import math

import jax
import jax.numpy as jnp
import numpy as np
from jax import lax
from jax.experimental import pallas as pl
from jax.experimental.pallas import tpu as pltpu
from jax.sharding import PartitionSpec as P

MESH = pl.DeviceIdType.MESH
LANES = 128
SECTIONS = 4
EMB_ROWS = 8


def unet_kernel(
    geometry,
    time_ref,
    freq_ref,
    gain_ref,
    taps_ref,
    film_ref,
    proj_ref,
    skip_ref,
    clips_ref,
    out_ref,
    time_smem,
    freq_vmem,
    gain_vmem,
    raw,
    raw_skip,
    raw_film,
    wt,
    skt,
    film_rows,
    film_col,
    gain_col,
    window,
    norm0,
    norm1,
    state,
    nrm,
    halo_l,
    halo_r,
    give,
    load_sem,
    take_sem,
    swap_send,
    swap_recv,
    deep_send,
    deep_recv,
    halo_send,
    halo_recv,
    own_send,
    own_recv,
    cut_send,
    cut_recv,
    side_send,
    side_recv,
    sib_send,
    sib_recv,
    film_send,
    film_recv,
    back_send,
    back_recv,
):
    C, chunks, frames = geometry
    pieces = 4 * C // LANES
    half = pieces // 2
    half_pix = chunks * LANES
    groups = frames // 2
    f32, bf16 = jnp.float32, jnp.bfloat16

    seg = lax.axis_index("segment")
    frame = lax.axis_index("frame")
    y_hi, core = seg // 2, seg % 2
    group, y_lo = frame // 2, frame % 2

    partner = (seg, group * 2 + 1 - y_lo)
    left = (seg, frame - 2)
    right = (seg, frame + 2)
    sibling = (y_hi * 2 + 1 - core, frame)
    across = ((1 - y_hi) * 2 + core, group * 2 + 1 - y_lo)
    has_left = group > 0
    has_right = group < groups - 1
    gathered = (1 - y_hi) * 2 + core
    relayed = (1 - y_hi) * 2 + 1 - core
    sib_own = y_hi * 2 + 1 - core
    early = jnp.logical_and(y_hi == 1, core == 0)
    second = jnp.logical_and(y_hi == 1, core == 1)
    patient = jnp.logical_and(y_hi == 0, core == 1)

    def remote(src, dst, send, recv, device):
        return pltpu.make_async_remote_copy(
            src_ref=src, dst_ref=dst, send_sem=send, recv_sem=recv, device_id=device, device_id_type=MESH
        )

    def at_left(action):
        pl.when(has_left)(action)

    def at_right(action):
        pl.when(has_right)(action)

    loads = [
        pltpu.make_async_copy(taps_ref.at[0, 0], raw.at[pl.ds(0, C)], load_sem.at[0]),
        pltpu.make_async_copy(taps_ref.at[0, 1], raw.at[pl.ds(C, C)], load_sem.at[1]),
        pltpu.make_async_copy(taps_ref.at[0, 2], raw.at[pl.ds(2 * C, C)], load_sem.at[2]),
        pltpu.make_async_copy(proj_ref.at[0], raw.at[pl.ds(3 * C, C)], load_sem.at[3]),
        pltpu.make_async_copy(film_ref.at[0], raw_film, load_sem.at[4]),
        pltpu.make_async_copy(skip_ref.at[0], raw_skip.at[pl.ds(0, C)], load_sem.at[5]),
        pltpu.make_async_copy(skip_ref.at[1], raw_skip.at[pl.ds(C, C)], load_sem.at[6]),
        pltpu.make_async_copy(time_ref, time_smem, load_sem.at[7]),
        pltpu.make_async_copy(freq_ref, freq_vmem, load_sem.at[8]),
        pltpu.make_async_copy(gain_ref, gain_vmem, load_sem.at[9]),
    ]
    for load in loads[:4]:
        load.start()

    def pixels(part, c):
        return pl.ds(pl.multiple_of(part * half_pix + c * LANES, LANES), LANES)

    def take(c):
        return pltpu.make_async_copy(
            clips_ref.at[0, 0, :, pixels(y_lo, c)], window.at[2 + y_lo, c], take_sem.at[c]
        )

    for c in range(chunks):
        take(c).start()
    for load in loads[4:]:
        load.start()

    barrier = pltpu.get_barrier_semaphore()
    at_left(lambda: pl.semaphore_signal(barrier, inc=1, device_id=left, device_id_type=MESH))
    at_right(lambda: pl.semaphore_signal(barrier, inc=1, device_id=right, device_id_type=MESH))
    for device in (partner, sibling, across):
        pl.semaphore_signal(barrier, inc=1, device_id=device, device_id_type=MESH)

    def turn():
        for load in loads[:4]:
            load.wait()
        for k in range(pieces):
            wt[seg, :, k * LANES : (k + 1) * LANES] = raw[k * LANES : (k + 1) * LANES, :].T

    source = jnp.logical_and(y_hi == 0, core == 0)
    pl.when(source)(turn)

    pl.semaphore_wait(barrier, 3 + has_left.astype(jnp.int32) + has_right.astype(jnp.int32))

    def swap(c):
        return remote(
            clips_ref.at[0, 0, :, pixels(1 - y_lo, c)],
            window.at[2 + y_lo, c],
            swap_send.at[c],
            swap_recv.at[c],
            partner,
        )

    def swap_in(c):
        return remote(
            clips_ref.at[0, 0, :, pixels(y_lo, c)],
            window.at[3 - y_lo, c],
            swap_send.at[c],
            swap_recv.at[c],
            partner,
        )

    def deep_left(kind, c):
        which = y_lo if kind == 0 else 1 - y_lo
        return remote(
            clips_ref.at[0, 0, :, pixels(y_lo, c)] if kind == 0 else window.at[2 + which, c], window.at[4 + which, c], deep_send.at[0, kind, c], deep_recv.at[0, kind, c], left
        )

    def deep_right(kind, c):
        which = y_lo if kind == 0 else 1 - y_lo
        return remote(
            clips_ref.at[0, 0, :, pixels(y_lo, c)] if kind == 0 else window.at[2 + which, c], window.at[which, c], deep_send.at[1, kind, c], deep_recv.at[1, kind, c], right
        )

    def block(index, q):
        return wt.at[index, :, pl.ds(pl.multiple_of(q * LANES, LANES), LANES)]

    def own_to_sibling(index):
        return remote(wt.at[index], wt.at[index], own_send.at[0], own_recv.at[0], sibling)

    def to_across(index, q):
        return remote(block(index, q), block(index, q), cut_send.at[q], cut_recv.at[q], across)

    def to_partner(index, q):
        return remote(block(index, q), block(index, q), side_send.at[q], side_recv.at[q], partner)

    def to_sibling(index, q):
        return remote(block(index, q), block(index, q), sib_send.at[q], sib_recv.at[q], sibling)

    def forward_cut(i):
        q = 2 * i + y_lo
        to_across(gathered, q).wait_recv()
        to_partner(gathered, q).start()
        to_sibling(gathered, q).start()

    def forward_side(i):
        q = 2 * i + 1 - y_lo
        to_partner(gathered, q).wait_recv()
        to_sibling(gathered, q).start()

    def cross_all():
        for q in range(pieces):
            to_across(seg, q).start()

    def cross():
        for i in range(half):
            to_across(seg, 2 * i + 1 - y_lo).start()

    pl.when(source)(cross_all)

    for c in range(chunks):
        swap(c).start()
        at_left(lambda: deep_left(0, c).start())
        at_right(lambda: deep_right(0, c).start())

    pl.when(jnp.logical_not(source))(turn)
    own_to_sibling(seg).start()

    for load in loads[7:]:
        load.wait()
    row = lax.broadcasted_iota(jnp.int32, (EMB_ROWS, 1), 0)
    when = jnp.zeros((EMB_ROWS, 1), jnp.int32)
    for m in range(SECTIONS):
        when = jnp.where(row == m, time_smem[m], when)
    angle = when.astype(f32) * freq_vmem[...]
    lane = lax.broadcasted_iota(jnp.int32, angle.shape, 1)
    emb = jnp.where(lane < C // 2, jnp.sin(angle), jnp.cos(angle)).astype(bf16)
    loads[4].wait()
    film_rows[seg] = jnp.dot(emb, raw_film[...], preferred_element_type=f32)

    def film_copy(index, which, device):
        return remote(film_rows.at[index], film_rows.at[index], film_send.at[which], film_recv.at[which], device)

    film_copy(seg, 0, sibling).start()
    film_copy(seg, 1, across).start()

    def pass_film():
        film_copy(gathered, 1, across).wait_recv()
        film_copy(gathered, 2, sibling).start()

    def column(values):
        return jnp.broadcast_to(values, (LANES, C)).T

    def modulate(s):
        mine = jnp.sum(jnp.where(row == seg, film_rows[s], 0.0), axis=0, keepdims=True)
        film_col[s] = column(1.0 + mine)

    for s in range(SECTIONS):
        gain_col[s] = column(gain_vmem[s : s + 1, :])

    @pl.when(jnp.logical_not(has_left))
    def _():
        halo_l[...] = jnp.zeros_like(halo_l)
        window[0:2] = jnp.zeros((2, chunks, C, LANES), bf16)

    @pl.when(jnp.logical_not(has_right))
    def _():
        halo_r[...] = jnp.zeros_like(halo_r)
        window[4:6] = jnp.zeros((2, chunks, C, LANES), bf16)

    def normed(values, s):
        meansq = jnp.sum(values * values, axis=0, keepdims=True) * (1.0 / C)
        return (values * lax.rsqrt(meansq + 1e-05) * gain_col[s]).astype(bf16)

    def norm_frame(j, c):
        norm0[j, c] = normed(window[j, c].astype(f32), 0)

    def own_norms(c, carry):
        take(c).wait()
        norm_frame(2 + y_lo, c)
        return carry

    lax.fori_loop(0, chunks, own_norms, 0)
    pl.when(jnp.logical_or(y_hi == 1, core == 1))(cross)

    for load in loads[5:7]:
        load.wait()
    for n in range(2):
        for k in range(C // LANES + 1):
            lo, hi = k * LANES, min((k + 1) * LANES, C)
            skt[n, :, lo:hi] = raw_skip[n * C + lo : n * C + hi, :].T

    direct = {0: (0, 1, 2), 1: (3, 4, 5), 2: (6, 7, 8), 3: (9,)}
    cut_second = {1: (0, 1), 2: (2, 3), 3: (4,)}
    side_second = {3: (0, 1)}
    cut_later = {2: (0, 1), 3: (2, 3, 4)}
    side_later = {1: (0, 1), 2: (2, 3), 3: (4,)}

    def arrive(c, carry):
        swap_in(c).wait_recv()
        at_left(lambda: deep_left(1, c).start())
        at_right(lambda: deep_right(1, c).start())
        norm_frame(3 - y_lo, c)
        for at in range(chunks):

            @pl.when(jnp.logical_and(early, c == at))
            def _():
                for q in direct.get(at, ()):
                    to_across(gathered, q).wait_recv()
                    to_sibling(gathered, q).start()

        at_left(lambda: deep_right(0, c).wait_recv())
        norm_frame(y_lo, c)
        at_right(lambda: deep_left(0, c).wait_recv())
        norm_frame(4 + y_lo, c)
        for at in range(chunks):

            @pl.when(jnp.logical_and(second, c == at))
            def _():
                for i in cut_second.get(at, ()):
                    forward_cut(i)
                for i in side_second.get(at, ()):
                    forward_side(i)

            @pl.when(jnp.logical_and(y_hi == 0, c == at))
            def _():
                for i in cut_later.get(at, ()):
                    forward_cut(i)

        return carry

    lax.fori_loop(0, chunks, arrive, 0)
    pass_film()

    def await_section(s):
        @pl.when(sib_own == s)
        def _():
            own_to_sibling(sib_own).wait_recv()
            film_copy(sib_own, 0, sibling).wait_recv()

        @pl.when(relayed == s)
        def _():
            for q in range(pieces):
                to_sibling(relayed, q).wait_recv()
            film_copy(relayed, 2, sibling).wait_recv()

        modulate(s)

    pad = jnp.zeros((4 * C - 3 * C - 2 * LANES, 2 * LANES), bf16)

    def section(s, normals, base, skip=None):
        taps = [jnp.concatenate(normals[t : t + 2], axis=1) for t in range(3)]
        mixed = jnp.dot(wt[s, :, : 8 * LANES], jnp.concatenate(taps + [pad], axis=0), preferred_element_type=f32)
        scale = film_col[s]
        hidden = jax.nn.silu(mixed * jnp.concatenate([scale, scale], axis=1)).astype(bf16)
        weights = wt[s, :, 7 * LANES :]
        fields = [pad, hidden]
        if skip is not None:
            weights = jnp.concatenate([weights, skt[s - 2]], axis=1)
            fields = fields + [skip]
        total = base.astype(f32) + jnp.dot(weights, jnp.concatenate(fields, axis=0), preferred_element_type=f32)
        return total.astype(bf16)

    def to_left(s, c):
        return remote(
            nrm.at[s - 2, 0, c], halo_r.at[s - 2, c], halo_send.at[0, s - 2, c], halo_recv.at[1, s - 2, c], left
        )

    def to_right(s, c):
        return remote(
            nrm.at[s - 2, 1, c], halo_l.at[s - 2, c], halo_send.at[1, s - 2, c], halo_recv.at[0, s - 2, c], right
        )

    def keep(result, s, c):
        state[s - 1, 0, c] = result[:, :LANES]
        state[s - 1, 1, c] = result[:, LANES:]
        values = result.astype(f32)
        nrm[s - 2, 0, c] = normed(values[:, :LANES], s)
        at_left(lambda: to_left(s, c).start())
        nrm[s - 2, 1, c] = normed(values[:, LANES:], s)
        at_right(lambda: to_right(s, c).start())

    def frames_of(ref, j, c):
        return jnp.concatenate([ref[j, c], ref[j + 1, c]], axis=1)

    await_section(0)

    def deep_step(c, carry):
        at_left(lambda: deep_right(1, c).wait_recv())
        norm_frame(1 - y_lo, c)
        at_right(lambda: deep_left(1, c).wait_recv())
        norm_frame(5 - y_lo, c)
        low = section(0, [norm0[j, c] for j in range(0, 4)], frames_of(window, 1, c))
        state[0, 0, c] = low[:, LANES:]
        values = low.astype(f32)
        norm1[0] = jnp.where(has_left, normed(values[:, :LANES], 1), jnp.zeros((C, LANES), bf16))
        norm1[1] = normed(values[:, LANES:], 1)
        high = section(0, [norm0[j, c] for j in range(2, 6)], frames_of(window, 3, c))
        state[0, 1, c] = high[:, :LANES]
        values = high.astype(f32)
        norm1[2] = normed(values[:, :LANES], 1)
        norm1[3] = jnp.where(has_right, normed(values[:, LANES:], 1), jnp.zeros((C, LANES), bf16))

        @pl.when(c == 0)
        def _():
            @pl.when(second)
            def _():
                for i in range(2, half):
                    forward_side(i)

            await_section(1)

        keep(section(1, [norm1[j] for j in range(4)], frames_of(state.at[0], 0, c)), 2, c)
        for at in range(chunks):

            @pl.when(jnp.logical_and(y_hi == 0, c == at))
            def _():
                for i in side_later.get(at, ()):
                    forward_side(i)

        return carry

    lax.fori_loop(0, chunks, deep_step, 0)

    def back_out(c):
        return remote(
            give.at[c], out_ref.at[0, 0, :, pixels(y_lo, c)], back_send.at[c], back_recv.at[c], partner
        )

    def back_in(c):
        return remote(
            give.at[c], out_ref.at[0, 0, :, pixels(1 - y_lo, c)], back_send.at[c], back_recv.at[c], partner
        )

    for s in (2, 3):
        await_section(s)

        def step(c, carry):
            at_left(lambda: to_right(s, c).wait_recv())
            at_right(lambda: to_left(s, c).wait_recv())
            normals = [halo_l[s - 2, c], nrm[s - 2, 0, c], nrm[s - 2, 1, c], halo_r[s - 2, c]]
            skip = frames_of(state.at[0], 0, c) if s == 2 else frames_of(window, 2, c)
            result = section(s, normals, frames_of(state.at[s - 1], 0, c), skip)
            if s == 2:
                keep(result, 3, c)
            else:
                give[c] = jnp.where(y_lo == 0, result[:, LANES:], result[:, :LANES])
                back_out(c).start()
                out_ref[0, 0, :, pixels(y_lo, c)] = jnp.where(y_lo == 0, result[:, :LANES], result[:, LANES:])
            return carry

        lax.fori_loop(0, chunks, step, 0)

    def finish(c, carry):
        swap(c).wait_send()
        for kind in range(2):
            at_left(lambda: deep_left(kind, c).wait_send())
            at_right(lambda: deep_right(kind, c).wait_send())
        for s in (2, 3):
            at_left(lambda: to_left(s, c).wait_send())
            at_right(lambda: to_right(s, c).wait_send())
        return carry

    lax.fori_loop(0, chunks, finish, 0)
    own_to_sibling(seg).wait_send()
    for i in range(half):
        to_across(seg, 2 * i + 1 - y_lo).wait_send()

    @pl.when(jnp.logical_and(y_hi == 0, core == 0))
    def _():
        for i in range(half):
            to_across(seg, 2 * i + y_lo).wait_send()

    @pl.when(jnp.logical_not(early))
    def _():
        for i in range(half):
            to_partner(gathered, 2 * i + y_lo).wait_send()

    for q in range(pieces):
        to_sibling(gathered, q).wait_send()
    film_copy(seg, 0, sibling).wait_send()
    film_copy(seg, 1, across).wait_send()
    film_copy(gathered, 2, sibling).wait_send()

    def returned(c, carry):
        back_out(c).wait_send()
        back_in(c).wait_recv()
        return carry

    lax.fori_loop(0, chunks, returned, 0)


def shards(geometry, clips, timesteps, gain, temporal_weight, film_weight, out_weight, skip_weight):
    C, chunks, frames = geometry
    pieces = 4 * C // LANES
    base = np.exp(-math.log(10000.0) * np.arange(C // 2) / (C // 2))
    freq = jnp.asarray(np.concatenate([base, base])[None, :].astype(np.float32))
    hbm = pl.BlockSpec(memory_space=pltpu.HBM)
    bf16, f32 = jnp.bfloat16, jnp.float32
    dma = pltpu.SemaphoreType.DMA
    flops = 2 * 22 * C * C * 2 * chunks * LANES
    return pl.pallas_call(
        functools.partial(unet_kernel, geometry),
        out_shape=pltpu.VMEM(clips.shape, bf16),
        in_specs=[hbm] * 8,
        out_specs=pl.BlockSpec(memory_space=pltpu.VMEM),
        scratch_shapes=[
            pltpu.SMEM(timesteps.shape, jnp.int32),
            pltpu.VMEM(freq.shape, f32),
            pltpu.VMEM(gain.shape, f32),
            pltpu.VMEM((4 * C, C), bf16),
            pltpu.VMEM((2 * C, C), bf16),
            pltpu.VMEM((C, C), bf16),
            pltpu.VMEM((SECTIONS, C, 4 * C), bf16),
            pltpu.VMEM((2, C, C), bf16),
            pltpu.VMEM((SECTIONS, EMB_ROWS, C), f32),
            pltpu.VMEM((SECTIONS, C, LANES), f32),
            pltpu.VMEM((SECTIONS, C, LANES), f32),
            pltpu.VMEM((6, chunks, C, LANES), bf16),
            pltpu.VMEM((6, chunks, C, LANES), bf16),
            pltpu.VMEM((4, C, LANES), bf16),
            pltpu.VMEM((3, 2, chunks, C, LANES), bf16),
            pltpu.VMEM((2, 2, chunks, C, LANES), bf16),
            pltpu.VMEM((2, chunks, C, LANES), bf16),
            pltpu.VMEM((2, chunks, C, LANES), bf16),
            pltpu.VMEM((chunks, C, LANES), bf16),
            dma((10,)),
            dma((chunks,)),
            dma((chunks,)),
            dma((chunks,)),
            dma((2, 2, chunks)),
            dma((2, 2, chunks)),
            dma((2, 2, chunks)),
            dma((2, 2, chunks)),
            dma((1,)),
            dma((1,)),
            dma((pieces,)),
            dma((pieces,)),
            dma((pieces,)),
            dma((pieces,)),
            dma((pieces,)),
            dma((pieces,)),
            dma((3,)),
            dma((3,)),
            dma((chunks,)),
            dma((chunks,)),
        ],
        compiler_params=pltpu.CompilerParams(
            collective_id=0, has_side_effects=True, vmem_limit_bytes=60 * 10**6
        ),
        cost_estimate=pl.CostEstimate(flops=flops, bytes_accessed=4 * clips.size, transcendentals=0),
        name="unet",
    )(timesteps, freq, gain, temporal_weight, film_weight, out_weight, skip_weight, clips)


def solution(mesh):
    frames = mesh.shape["frame"]

    def run(clips, *rest):
        _, _, C, pix = clips.shape
        geometry = (C, pix // 2 // LANES, frames)
        return shards(geometry, clips, *rest)

    placed = (
        P("segment", "frame", None, None),
        P(),
        P(),
        P("segment", None, None, None),
        P("segment", None, None),
        P("segment", None, None),
        P(),
    )
    return jax.shard_map(
        run,
        mesh=mesh,
        in_specs=placed,
        out_specs=P("segment", "frame", None, None),
        check_vma=False,
    )
```

```python
import functools
import math

import jax
import jax.numpy as jnp
import numpy as np
from jax import lax
from jax.experimental import pallas as pl
from jax.experimental.pallas import tpu as pltpu
from jax.sharding import PartitionSpec as P

MESH = pl.DeviceIdType.MESH
LANES = 128
SECTIONS = 4
EMB_ROWS = 8
SHARED = 4


def unet_kernel(
    geometry,
    time_ref,
    freq_ref,
    gain_ref,
    taps_ref,
    film_ref,
    proj_ref,
    skip_ref,
    clips_ref,
    out_ref,
    time_smem,
    freq_vmem,
    gain_vmem,
    raw,
    raw_skip,
    raw_film,
    wt,
    skt,
    film_rows,
    film_col,
    gain_col,
    window,
    norm0,
    norm1,
    state,
    nrm,
    halo_l,
    halo_r,
    give,
    load_sem,
    take_sem,
    swap_send,
    swap_recv,
    deep_send,
    deep_recv,
    halo_send,
    halo_recv,
    own_send,
    own_recv,
    cut_send,
    cut_recv,
    side_send,
    side_recv,
    sib_send,
    sib_recv,
    film_send,
    film_recv,
    back_send,
    back_recv,
):
    C, chunks, frames = geometry
    pieces = 4 * C // LANES
    direct = pieces - SHARED
    half_pix = chunks * LANES
    groups = frames // 2
    f32, bf16 = jnp.float32, jnp.bfloat16

    seg = lax.axis_index("segment")
    frame = lax.axis_index("frame")
    y_hi, core = seg // 2, seg % 2
    group, y_lo = frame // 2, frame % 2

    partner = (seg, group * 2 + 1 - y_lo)
    left = (seg, frame - 2)
    right = (seg, frame + 2)
    sibling = (y_hi * 2 + 1 - core, frame)
    across = ((1 - y_hi) * 2 + core, group * 2 + 1 - y_lo)
    x_step = 16 if frames >= 32 else 2
    spread = frames // x_step
    x_par = (frame // x_step) % 2
    turn_x = jnp.where((frame % x_step) // 2 == x_step // 2 - 1, 1, spread - 1)
    ahead = (seg, (frame + x_step * turn_x) % frames)
    behind = (seg, (frame + x_step * (spread - turn_x)) % frames)
    has_left = group > 0
    has_right = group < groups - 1
    gathered = (1 - y_hi) * 2 + core
    relayed = (1 - y_hi) * 2 + 1 - core
    sib_own = y_hi * 2 + 1 - core
    early = jnp.logical_and(y_hi == 1, core == 0)
    second = jnp.logical_and(y_hi == 1, core == 1)
    patient = jnp.logical_and(y_hi == 0, core == 1)

    def remote(src, dst, send, recv, device):
        return pltpu.make_async_remote_copy(
            src_ref=src, dst_ref=dst, send_sem=send, recv_sem=recv, device_id=device, device_id_type=MESH
        )

    def at_left(action):
        pl.when(has_left)(action)

    def at_right(action):
        pl.when(has_right)(action)

    loads = [
        pltpu.make_async_copy(taps_ref.at[0, 0], raw.at[pl.ds(0, C)], load_sem.at[0]),
        pltpu.make_async_copy(taps_ref.at[0, 1], raw.at[pl.ds(C, C)], load_sem.at[1]),
        pltpu.make_async_copy(taps_ref.at[0, 2], raw.at[pl.ds(2 * C, C)], load_sem.at[2]),
        pltpu.make_async_copy(proj_ref.at[0], raw.at[pl.ds(3 * C, C)], load_sem.at[3]),
        pltpu.make_async_copy(film_ref.at[0], raw_film, load_sem.at[4]),
        pltpu.make_async_copy(skip_ref.at[0], raw_skip.at[pl.ds(0, C)], load_sem.at[5]),
        pltpu.make_async_copy(skip_ref.at[1], raw_skip.at[pl.ds(C, C)], load_sem.at[6]),
        pltpu.make_async_copy(time_ref, time_smem, load_sem.at[7]),
        pltpu.make_async_copy(freq_ref, freq_vmem, load_sem.at[8]),
        pltpu.make_async_copy(gain_ref, gain_vmem, load_sem.at[9]),
    ]
    for load in loads[:4]:
        load.start()

    def pixels(part, c):
        return pl.ds(pl.multiple_of(part * half_pix + c * LANES, LANES), LANES)

    def take(c):
        return pltpu.make_async_copy(
            clips_ref.at[0, 0, :, pixels(y_lo, c)], window.at[2 + y_lo, c], take_sem.at[c]
        )

    for c in range(chunks):
        take(c).start()
    for load in loads[4:]:
        load.start()

    barrier = pltpu.get_barrier_semaphore()
    at_left(lambda: pl.semaphore_signal(barrier, inc=1, device_id=left, device_id_type=MESH))
    at_right(lambda: pl.semaphore_signal(barrier, inc=1, device_id=right, device_id_type=MESH))
    for device in (partner, sibling, across):
        pl.semaphore_signal(barrier, inc=1, device_id=device, device_id_type=MESH)

    @pl.when(early)
    def _():
        for device in (ahead, behind):
            pl.semaphore_signal(barrier, inc=1, device_id=device, device_id_type=MESH)

    def turn():
        for load in loads[:4]:
            load.wait()
        for k in range(pieces):
            wt[seg, :, k * LANES : (k + 1) * LANES] = raw[k * LANES : (k + 1) * LANES, :].T

    source = jnp.logical_and(y_hi == 0, core == 0)
    pl.when(source)(turn)

    pl.semaphore_wait(barrier, 3 + 2 * early.astype(jnp.int32) + has_left.astype(jnp.int32) + has_right.astype(jnp.int32))

    def swap(c):
        return remote(
            clips_ref.at[0, 0, :, pixels(1 - y_lo, c)],
            window.at[2 + y_lo, c],
            swap_send.at[c],
            swap_recv.at[c],
            partner,
        )

    def swap_in(c):
        return remote(
            clips_ref.at[0, 0, :, pixels(y_lo, c)],
            window.at[3 - y_lo, c],
            swap_send.at[c],
            swap_recv.at[c],
            partner,
        )

    def deep_left(kind, c):
        which = y_lo if kind == 0 else 1 - y_lo
        return remote(
            clips_ref.at[0, 0, :, pixels(y_lo, c)] if kind == 0 else window.at[2 + which, c], window.at[4 + which, c], deep_send.at[0, kind, c], deep_recv.at[0, kind, c], left
        )

    def deep_right(kind, c):
        which = y_lo if kind == 0 else 1 - y_lo
        return remote(
            clips_ref.at[0, 0, :, pixels(y_lo, c)] if kind == 0 else window.at[2 + which, c], window.at[which, c], deep_send.at[1, kind, c], deep_recv.at[1, kind, c], right
        )

    def block(index, q):
        return wt.at[index, :, pl.ds(pl.multiple_of(q * LANES, LANES), LANES)]

    def own_to_sibling(index):
        return remote(wt.at[index], wt.at[index], own_send.at[0], own_recv.at[0], sibling)

    def to_across(index, q):
        return remote(block(index, q), block(index, q), cut_send.at[q], cut_recv.at[q], across)

    def to_partner(index, q):
        return remote(block(index, q), block(index, q), side_send.at[q], side_recv.at[q], partner)

    def to_sibling(index, q):
        return remote(block(index, q), block(index, q), sib_send.at[q], sib_recv.at[q], sibling)

    def to_ahead(index, q):
        return remote(block(index, q), block(index, q), side_send.at[q], side_recv.at[q], ahead)

    def order(parity, i):
        return i + parity * (pieces - 1 - 2 * i)

    def first_cut(i):
        q = order(x_par, i)
        to_across(gathered, q).wait_recv()
        if i < SHARED:
            to_ahead(gathered, q).start()
        to_sibling(gathered, q).start()

    def first_side(i):
        q = order(1 - x_par, i)
        to_ahead(gathered, q).wait_recv()
        to_sibling(gathered, q).start()

    def forward_cut(i):
        q = order(y_lo, i)
        to_across(gathered, q).wait_recv()
        if i < SHARED:
            to_partner(gathered, q).start()
        to_sibling(gathered, q).start()

    def forward_side(i):
        q = order(1 - y_lo, i)
        to_partner(gathered, q).wait_recv()
        to_sibling(gathered, q).start()

    def cross_first():
        for i in range(direct):
            to_across(seg, order(x_par, i)).start()

    def cross():
        for i in range(direct):
            to_across(seg, order(1 - y_lo, i)).start()

    shares = range(SHARED)
    pl.when(source)(cross_first)

    for c in range(chunks):
        swap(c).start()
        at_left(lambda: deep_left(0, c).start())
        at_right(lambda: deep_right(0, c).start())

    pl.when(jnp.logical_not(source))(turn)
    own_to_sibling(seg).start()

    for load in loads[7:]:
        load.wait()
    row = lax.broadcasted_iota(jnp.int32, (EMB_ROWS, 1), 0)
    when = jnp.zeros((EMB_ROWS, 1), jnp.int32)
    for m in range(SECTIONS):
        when = jnp.where(row == m, time_smem[m], when)
    angle = when.astype(f32) * freq_vmem[...]
    lane = lax.broadcasted_iota(jnp.int32, angle.shape, 1)
    emb = jnp.where(lane < C // 2, jnp.sin(angle), jnp.cos(angle)).astype(bf16)
    loads[4].wait()
    film_rows[seg] = jnp.dot(emb, raw_film[...], preferred_element_type=f32)

    def film_copy(index, which, device):
        return remote(film_rows.at[index], film_rows.at[index], film_send.at[which], film_recv.at[which], device)

    film_copy(seg, 0, sibling).start()
    film_copy(seg, 1, across).start()

    def pass_film():
        film_copy(gathered, 1, across).wait_recv()
        film_copy(gathered, 2, sibling).start()

    def column(values):
        return jnp.broadcast_to(values, (LANES, C)).T

    def modulate(s):
        mine = jnp.sum(jnp.where(row == seg, film_rows[s], 0.0), axis=0, keepdims=True)
        film_col[s] = column(1.0 + mine)

    for s in range(SECTIONS):
        gain_col[s] = column(gain_vmem[s : s + 1, :])

    @pl.when(jnp.logical_not(has_left))
    def _():
        halo_l[...] = jnp.zeros_like(halo_l)
        window[0:2] = jnp.zeros((2, chunks, C, LANES), bf16)

    @pl.when(jnp.logical_not(has_right))
    def _():
        halo_r[...] = jnp.zeros_like(halo_r)
        window[4:6] = jnp.zeros((2, chunks, C, LANES), bf16)

    def normed(values, s):
        meansq = jnp.sum(values * values, axis=0, keepdims=True) * (1.0 / C)
        return (values * lax.rsqrt(meansq + 1e-05) * gain_col[s]).astype(bf16)

    def norm_frame(j, c):
        norm0[j, c] = normed(window[j, c].astype(f32), 0)

    def own_norms(c, carry):
        take(c).wait()
        norm_frame(2 + y_lo, c)
        return carry

    lax.fori_loop(0, chunks, own_norms, 0)
    pl.when(early)(cross)

    for load in loads[5:7]:
        load.wait()
    for n in range(2):
        for k in range(C // LANES + 1):
            lo, hi = k * LANES, min((k + 1) * LANES, C)
            skt[n, :, lo:hi] = raw_skip[n * C + lo : n * C + hi, :].T

    first_plan = {0: (0, 1, 2), 1: (3, 4), 2: range(5, direct)}
    later_plan = {2: (0, 1, 2), 3: (3, 4, 5)}

    def arrive(c, carry):
        swap_in(c).wait_recv()
        at_left(lambda: deep_left(1, c).start())
        at_right(lambda: deep_right(1, c).start())
        norm_frame(3 - y_lo, c)
        for at in range(chunks):

            @pl.when(jnp.logical_and(early, c == at))
            def _():
                for i in first_plan.get(at, ()):
                    first_cut(i)
                if at == 2:
                    for i in shares:
                        first_side(i)

        pl.when(jnp.logical_and(patient, c == 0))(cross)
        at_left(lambda: deep_right(0, c).wait_recv())
        norm_frame(y_lo, c)
        at_right(lambda: deep_left(0, c).wait_recv())
        norm_frame(4 + y_lo, c)
        for at in range(chunks):

            @pl.when(jnp.logical_and(source, c == at))
            def _():
                for i in later_plan.get(at, ()):
                    forward_cut(i)

        @pl.when(jnp.logical_and(second, c == chunks - 1))
        def _():
            cross()
            for i in shares:
                forward_cut(i)

        return carry

    lax.fori_loop(0, chunks, arrive, 0)
    pass_film()

    def await_section(s):
        @pl.when(sib_own == s)
        def _():
            own_to_sibling(sib_own).wait_recv()
            film_copy(sib_own, 0, sibling).wait_recv()

        @pl.when(relayed == s)
        def _():
            for q in range(pieces):
                to_sibling(relayed, q).wait_recv()
            film_copy(relayed, 2, sibling).wait_recv()

        modulate(s)

    def section(s, normals, base, skip=None, parts=1):
        count = len(normals) - 2
        pad = jnp.zeros((4 * C - 3 * C - 2 * LANES, count * LANES), bf16)
        taps = [jnp.concatenate(normals[t : t + count], axis=1) for t in range(3)]
        stacked = jnp.concatenate(taps + [pad], axis=0)
        hidden = []
        for part in range(parts):
            rows = slice(part * C // parts, (part + 1) * C // parts)
            mixed = jnp.dot(wt[s, rows, : 8 * LANES], stacked, preferred_element_type=f32)
            scale = jnp.concatenate([film_col[s, rows]] * count, axis=1)
            hidden.append(jax.nn.silu(mixed * scale).astype(bf16))
        weights = wt[s, :, 7 * LANES :]
        fields = [pad] + hidden
        if skip is not None:
            weights = jnp.concatenate([weights, skt[s - 2]], axis=1)
            fields = fields + [skip]
        total = base.astype(f32) + jnp.dot(weights, jnp.concatenate(fields, axis=0), preferred_element_type=f32)
        return total.astype(bf16)

    def to_left(s, c):
        return remote(
            nrm.at[s - 2, 0, c], halo_r.at[s - 2, c], halo_send.at[0, s - 2, c], halo_recv.at[1, s - 2, c], left
        )

    def to_right(s, c):
        return remote(
            nrm.at[s - 2, 1, c], halo_l.at[s - 2, c], halo_send.at[1, s - 2, c], halo_recv.at[0, s - 2, c], right
        )

    def keep(result, s, c):
        state[s - 1, 0, c] = result[:, :LANES]
        state[s - 1, 1, c] = result[:, LANES:]
        values = result.astype(f32)
        nrm[s - 2, 0, c] = normed(values[:, :LANES], s)
        at_left(lambda: to_left(s, c).start())
        nrm[s - 2, 1, c] = normed(values[:, LANES:], s)
        at_right(lambda: to_right(s, c).start())

    def frames_of(ref, j, c):
        return jnp.concatenate([ref[j, c], ref[j + 1, c]], axis=1)

    await_section(0)

    def deep_step(c, carry):
        at_left(lambda: deep_right(1, c).wait_recv())
        norm_frame(1 - y_lo, c)
        at_right(lambda: deep_left(1, c).wait_recv())
        norm_frame(5 - y_lo, c)
        base = jnp.concatenate([window[j, c] for j in range(1, 5)], axis=1)
        wide = section(0, [norm0[j, c] for j in range(6)], base)
        state[0, 0, c] = wide[:, LANES : 2 * LANES]
        state[0, 1, c] = wide[:, 2 * LANES : 3 * LANES]
        values = wide.astype(f32)
        nothing = jnp.zeros((C, LANES), bf16)
        norm1[0] = jnp.where(has_left, normed(values[:, :LANES], 1), nothing)
        norm1[1] = normed(values[:, LANES : 2 * LANES], 1)
        norm1[2] = normed(values[:, 2 * LANES : 3 * LANES], 1)
        norm1[3] = jnp.where(has_right, normed(values[:, 3 * LANES :], 1), nothing)

        @pl.when(c == 0)
        def _():
            @pl.when(second)
            def _():
                for i in range(SHARED, direct):
                    forward_cut(i)
                for i in shares:
                    forward_side(i)

            await_section(1)

        keep(section(1, [norm1[j] for j in range(4)], frames_of(state.at[0], 0, c), parts=2), 2, c)
        @pl.when(jnp.logical_and(source, c == 0))
        def _():
            for i in range(6, direct):
                forward_cut(i)

        @pl.when(jnp.logical_and(source, c == 1))
        def _():
            for i in shares:
                forward_side(i)

        return carry

    lax.fori_loop(0, chunks, deep_step, 0)

    def back_out(c):
        return remote(
            give.at[c], out_ref.at[0, 0, :, pixels(y_lo, c)], back_send.at[c], back_recv.at[c], partner
        )

    def back_in(c):
        return remote(
            give.at[c], out_ref.at[0, 0, :, pixels(1 - y_lo, c)], back_send.at[c], back_recv.at[c], partner
        )

    for s in (2, 3):
        await_section(s)

        def step(c, carry):
            at_left(lambda: to_right(s, c).wait_recv())
            at_right(lambda: to_left(s, c).wait_recv())
            normals = [halo_l[s - 2, c], nrm[s - 2, 0, c], nrm[s - 2, 1, c], halo_r[s - 2, c]]
            skip = frames_of(state.at[0], 0, c) if s == 2 else frames_of(window, 2, c)
            result = section(s, normals, frames_of(state.at[s - 1], 0, c), skip, parts=2)
            if s == 2:
                keep(result, 3, c)

                @pl.when(jnp.logical_and(patient, c == 0))
                def _():
                    for i in shares:
                        forward_cut(i)

                @pl.when(jnp.logical_and(patient, c == 1))
                def _():
                    for i in range(SHARED, direct):
                        forward_cut(i)

                @pl.when(jnp.logical_and(patient, c == 2))
                def _():
                    for i in shares:
                        forward_side(i)

            else:
                give[c] = jnp.where(y_lo == 0, result[:, LANES:], result[:, :LANES])
                back_out(c).start()
                out_ref[0, 0, :, pixels(y_lo, c)] = jnp.where(y_lo == 0, result[:, :LANES], result[:, LANES:])
            return carry

        lax.fori_loop(0, chunks, step, 0)

    def finish(c, carry):
        swap(c).wait_send()
        for kind in range(2):
            at_left(lambda: deep_left(kind, c).wait_send())
            at_right(lambda: deep_right(kind, c).wait_send())
        for s in (2, 3):
            at_left(lambda: to_left(s, c).wait_send())
            at_right(lambda: to_right(s, c).wait_send())
        return carry

    lax.fori_loop(0, chunks, finish, 0)
    own_to_sibling(seg).wait_send()
    @pl.when(source)
    def _():
        for i in range(direct):
            to_across(seg, order(x_par, i)).wait_send()

    @pl.when(jnp.logical_not(source))
    def _():
        for i in range(direct):
            to_across(seg, order(1 - y_lo, i)).wait_send()

    @pl.when(early)
    def _():
        for i in shares:
            to_ahead(gathered, order(x_par, i)).wait_send()

    @pl.when(jnp.logical_not(early))
    def _():
        for i in shares:
            to_partner(gathered, order(y_lo, i)).wait_send()

    for q in range(pieces):
        to_sibling(gathered, q).wait_send()
    film_copy(seg, 0, sibling).wait_send()
    film_copy(seg, 1, across).wait_send()
    film_copy(gathered, 2, sibling).wait_send()

    def returned(c, carry):
        back_out(c).wait_send()
        back_in(c).wait_recv()
        return carry

    lax.fori_loop(0, chunks, returned, 0)


def shards(geometry, clips, timesteps, gain, temporal_weight, film_weight, out_weight, skip_weight):
    C, chunks, frames = geometry
    pieces = 4 * C // LANES
    base = np.exp(-math.log(10000.0) * np.arange(C // 2) / (C // 2))
    freq = jnp.asarray(np.concatenate([base, base])[None, :].astype(np.float32))
    hbm = pl.BlockSpec(memory_space=pltpu.HBM)
    bf16, f32 = jnp.bfloat16, jnp.float32
    dma = pltpu.SemaphoreType.DMA
    flops = 2 * 22 * C * C * 2 * chunks * LANES
    return pl.pallas_call(
        functools.partial(unet_kernel, geometry),
        out_shape=pltpu.VMEM(clips.shape, bf16),
        in_specs=[hbm] * 8,
        out_specs=pl.BlockSpec(memory_space=pltpu.VMEM),
        scratch_shapes=[
            pltpu.SMEM(timesteps.shape, jnp.int32),
            pltpu.VMEM(freq.shape, f32),
            pltpu.VMEM(gain.shape, f32),
            pltpu.VMEM((4 * C, C), bf16),
            pltpu.VMEM((2 * C, C), bf16),
            pltpu.VMEM((C, C), bf16),
            pltpu.VMEM((SECTIONS, C, 4 * C), bf16),
            pltpu.VMEM((2, C, C), bf16),
            pltpu.VMEM((SECTIONS, EMB_ROWS, C), f32),
            pltpu.VMEM((SECTIONS, C, LANES), f32),
            pltpu.VMEM((SECTIONS, C, LANES), f32),
            pltpu.VMEM((6, chunks, C, LANES), bf16),
            pltpu.VMEM((6, chunks, C, LANES), bf16),
            pltpu.VMEM((4, C, LANES), bf16),
            pltpu.VMEM((3, 2, chunks, C, LANES), bf16),
            pltpu.VMEM((2, 2, chunks, C, LANES), bf16),
            pltpu.VMEM((2, chunks, C, LANES), bf16),
            pltpu.VMEM((2, chunks, C, LANES), bf16),
            pltpu.VMEM((chunks, C, LANES), bf16),
            dma((10,)),
            dma((chunks,)),
            dma((chunks,)),
            dma((chunks,)),
            dma((2, 2, chunks)),
            dma((2, 2, chunks)),
            dma((2, 2, chunks)),
            dma((2, 2, chunks)),
            dma((1,)),
            dma((1,)),
            dma((pieces,)),
            dma((pieces,)),
            dma((pieces,)),
            dma((pieces,)),
            dma((pieces,)),
            dma((pieces,)),
            dma((3,)),
            dma((3,)),
            dma((chunks,)),
            dma((chunks,)),
        ],
        compiler_params=pltpu.CompilerParams(
            collective_id=0, has_side_effects=True, vmem_limit_bytes=60 * 10**6
        ),
        cost_estimate=pl.CostEstimate(flops=flops, bytes_accessed=4 * clips.size, transcendentals=0),
        name="unet",
    )(timesteps, freq, gain, temporal_weight, film_weight, out_weight, skip_weight, clips)


def solution(mesh):
    frames = mesh.shape["frame"]

    def run(clips, *rest):
        _, _, C, pix = clips.shape
        geometry = (C, pix // 2 // LANES, frames)
        return shards(geometry, clips, *rest)

    placed = (
        P("segment", "frame", None, None),
        P(),
        P(),
        P("segment", None, None, None),
        P("segment", None, None),
        P("segment", None, None),
        P(),
    )
    return jax.shard_map(
        run,
        mesh=mesh,
        in_specs=placed,
        out_specs=P("segment", "frame", None, None),
        check_vma=False,
    )
```

```python
import functools
import math

import jax
import jax.numpy as jnp
import numpy as np
from jax import lax
from jax.experimental import pallas as pl
from jax.experimental.pallas import tpu as pltpu
from jax.sharding import PartitionSpec as P

MESH = pl.DeviceIdType.MESH
LANES = 128
SECTIONS = 4
EMB_ROWS = 8
SHARED = 4


def unet_kernel(
    geometry,
    time_ref,
    freq_ref,
    gain_ref,
    taps_ref,
    film_ref,
    proj_ref,
    skip_ref,
    clips_ref,
    out_ref,
    time_smem,
    freq_vmem,
    gain_vmem,
    raw,
    raw_skip,
    raw_film,
    wt,
    skt,
    film_rows,
    film_col,
    gain_col,
    window,
    norm0,
    norm1,
    state,
    nrm,
    halo_l,
    halo_r,
    give,
    load_sem,
    take_sem,
    swap_send,
    swap_recv,
    deep_send,
    deep_recv,
    halo_send,
    halo_recv,
    own_send,
    own_recv,
    cut_send,
    cut_recv,
    side_send,
    side_recv,
    sib_send,
    sib_recv,
    film_send,
    film_recv,
    back_send,
    back_recv,
):
    C, chunks, frames = geometry
    pieces = 4 * C // LANES
    direct = pieces - SHARED
    half_pix = chunks * LANES
    groups = frames // 2
    f32, bf16 = jnp.float32, jnp.bfloat16

    seg = lax.axis_index("segment")
    frame = lax.axis_index("frame")
    y_hi, core = seg // 2, seg % 2
    group, y_lo = frame // 2, frame % 2

    partner = (seg, group * 2 + 1 - y_lo)
    left = (seg, frame - 2)
    right = (seg, frame + 2)
    sibling = (y_hi * 2 + 1 - core, frame)
    across = ((1 - y_hi) * 2 + core, group * 2 + 1 - y_lo)
    x_step = 16 if frames >= 32 else 2
    spread = frames // x_step
    x_par = (frame // x_step) % 2
    turn_x = jnp.where((frame % x_step) // 2 == x_step // 2 - 1, 1, spread - 1)
    ahead = (seg, (frame + x_step * turn_x) % frames)
    behind = (seg, (frame + x_step * (spread - turn_x)) % frames)
    has_left = group > 0
    has_right = group < groups - 1
    gathered = (1 - y_hi) * 2 + core
    relayed = (1 - y_hi) * 2 + 1 - core
    sib_own = y_hi * 2 + 1 - core
    early = jnp.logical_and(y_hi == 1, core == 0)
    second = jnp.logical_and(y_hi == 1, core == 1)
    patient = jnp.logical_and(y_hi == 0, core == 1)

    def remote(src, dst, send, recv, device):
        return pltpu.make_async_remote_copy(
            src_ref=src, dst_ref=dst, send_sem=send, recv_sem=recv, device_id=device, device_id_type=MESH
        )

    def at_left(action):
        pl.when(has_left)(action)

    def at_right(action):
        pl.when(has_right)(action)

    loads = [
        pltpu.make_async_copy(taps_ref.at[0, 0], raw.at[pl.ds(0, C)], load_sem.at[0]),
        pltpu.make_async_copy(taps_ref.at[0, 1], raw.at[pl.ds(C, C)], load_sem.at[1]),
        pltpu.make_async_copy(taps_ref.at[0, 2], raw.at[pl.ds(2 * C, C)], load_sem.at[2]),
        pltpu.make_async_copy(proj_ref.at[0], raw.at[pl.ds(3 * C, C)], load_sem.at[3]),
        pltpu.make_async_copy(film_ref.at[0], raw_film, load_sem.at[4]),
        pltpu.make_async_copy(skip_ref.at[0], raw_skip.at[pl.ds(0, C)], load_sem.at[5]),
        pltpu.make_async_copy(skip_ref.at[1], raw_skip.at[pl.ds(C, C)], load_sem.at[6]),
        pltpu.make_async_copy(time_ref, time_smem, load_sem.at[7]),
        pltpu.make_async_copy(freq_ref, freq_vmem, load_sem.at[8]),
        pltpu.make_async_copy(gain_ref, gain_vmem, load_sem.at[9]),
    ]
    for load in loads[:4]:
        load.start()

    def pixels(part, c):
        return pl.ds(pl.multiple_of(part * half_pix + c * LANES, LANES), LANES)

    def take(c):
        return pltpu.make_async_copy(
            clips_ref.at[0, 0, :, pixels(y_lo, c)], window.at[2 + y_lo, c], take_sem.at[c]
        )

    for c in range(chunks):
        take(c).start()
    for load in loads[4:]:
        load.start()

    barrier = pltpu.get_barrier_semaphore()
    at_left(lambda: pl.semaphore_signal(barrier, inc=1, device_id=left, device_id_type=MESH))
    at_right(lambda: pl.semaphore_signal(barrier, inc=1, device_id=right, device_id_type=MESH))
    for device in (partner, sibling, across):
        pl.semaphore_signal(barrier, inc=1, device_id=device, device_id_type=MESH)

    @pl.when(early)
    def _():
        for device in (ahead, behind):
            pl.semaphore_signal(barrier, inc=1, device_id=device, device_id_type=MESH)

    def turn():
        for load in loads[:4]:
            load.wait()
        for k in range(pieces):
            wt[seg, :, k * LANES : (k + 1) * LANES] = raw[k * LANES : (k + 1) * LANES, :].T

    source = jnp.logical_and(y_hi == 0, core == 0)
    pl.when(source)(turn)

    pl.semaphore_wait(barrier, 3 + 2 * early.astype(jnp.int32) + has_left.astype(jnp.int32) + has_right.astype(jnp.int32))

    def swap(c):
        return remote(
            clips_ref.at[0, 0, :, pixels(1 - y_lo, c)],
            window.at[2 + y_lo, c],
            swap_send.at[c],
            swap_recv.at[c],
            partner,
        )

    def swap_in(c):
        return remote(
            clips_ref.at[0, 0, :, pixels(y_lo, c)],
            window.at[3 - y_lo, c],
            swap_send.at[c],
            swap_recv.at[c],
            partner,
        )

    def deep_left(kind, c):
        which = y_lo if kind == 0 else 1 - y_lo
        return remote(
            clips_ref.at[0, 0, :, pixels(y_lo, c)] if kind == 0 else window.at[2 + which, c], window.at[4 + which, c], deep_send.at[0, kind, c], deep_recv.at[0, kind, c], left
        )

    def deep_right(kind, c):
        which = y_lo if kind == 0 else 1 - y_lo
        return remote(
            clips_ref.at[0, 0, :, pixels(y_lo, c)] if kind == 0 else window.at[2 + which, c], window.at[which, c], deep_send.at[1, kind, c], deep_recv.at[1, kind, c], right
        )

    def block(index, q):
        return wt.at[index, :, pl.ds(pl.multiple_of(q * LANES, LANES), LANES)]

    def own_to_sibling(index):
        return remote(wt.at[index], wt.at[index], own_send.at[0], own_recv.at[0], sibling)

    def to_across(index, q):
        return remote(block(index, q), block(index, q), cut_send.at[q], cut_recv.at[q], across)

    def to_partner(index, q):
        return remote(block(index, q), block(index, q), side_send.at[q], side_recv.at[q], partner)

    def to_sibling(index, q):
        return remote(block(index, q), block(index, q), sib_send.at[q], sib_recv.at[q], sibling)

    def to_ahead(index, q):
        return remote(block(index, q), block(index, q), side_send.at[q], side_recv.at[q], ahead)

    def order(parity, i):
        return i + parity * (pieces - 1 - 2 * i)

    def first_cut(i):
        q = order(x_par, i)
        to_across(gathered, q).wait_recv()
        if i < SHARED:
            to_ahead(gathered, q).start()
        to_sibling(gathered, q).start()

    def first_side(i):
        q = order(1 - x_par, i)
        to_ahead(gathered, q).wait_recv()
        to_sibling(gathered, q).start()

    def forward_cut(i):
        q = order(y_lo, i)
        to_across(gathered, q).wait_recv()
        if i < SHARED:
            to_partner(gathered, q).start()
        to_sibling(gathered, q).start()

    def forward_side(i):
        q = order(1 - y_lo, i)
        to_partner(gathered, q).wait_recv()
        to_sibling(gathered, q).start()

    def cross_first():
        for i in range(direct):
            to_across(seg, order(x_par, i)).start()

    def cross():
        for i in range(direct):
            to_across(seg, order(1 - y_lo, i)).start()

    shares = range(SHARED)
    pl.when(source)(cross_first)

    for c in range(chunks):
        swap(c).start()
        at_left(lambda: deep_left(0, c).start())
        at_right(lambda: deep_right(0, c).start())

    pl.when(jnp.logical_not(source))(turn)
    pl.when(y_hi == 0)(lambda: own_to_sibling(seg).start())

    for load in loads[7:]:
        load.wait()
    row = lax.broadcasted_iota(jnp.int32, (EMB_ROWS, 1), 0)
    when = jnp.zeros((EMB_ROWS, 1), jnp.int32)
    for m in range(SECTIONS):
        when = jnp.where(row == m, time_smem[m], when)
    angle = when.astype(f32) * freq_vmem[...]
    lane = lax.broadcasted_iota(jnp.int32, angle.shape, 1)
    emb = jnp.where(lane < C // 2, jnp.sin(angle), jnp.cos(angle)).astype(bf16)
    loads[4].wait()
    film_rows[seg] = jnp.dot(emb, raw_film[...], preferred_element_type=f32)

    def film_copy(index, which, device):
        return remote(film_rows.at[index], film_rows.at[index], film_send.at[which], film_recv.at[which], device)

    film_copy(seg, 0, sibling).start()
    film_copy(seg, 1, across).start()

    def pass_film():
        film_copy(gathered, 1, across).wait_recv()
        film_copy(gathered, 2, sibling).start()

    def column(values):
        return jnp.broadcast_to(values, (LANES, C)).T

    def modulate(s):
        mine = jnp.sum(jnp.where(row == seg, film_rows[s], 0.0), axis=0, keepdims=True)
        film_col[s] = column(1.0 + mine)

    for s in range(SECTIONS):
        gain_col[s] = column(gain_vmem[s : s + 1, :])

    @pl.when(jnp.logical_not(has_left))
    def _():
        halo_l[...] = jnp.zeros_like(halo_l)
        window[0:2] = jnp.zeros((2, chunks, C, LANES), bf16)

    @pl.when(jnp.logical_not(has_right))
    def _():
        halo_r[...] = jnp.zeros_like(halo_r)
        window[4:6] = jnp.zeros((2, chunks, C, LANES), bf16)

    def normed(values, s):
        meansq = jnp.sum(values * values, axis=0, keepdims=True) * (1.0 / C)
        return (values * lax.rsqrt(meansq + 1e-05) * gain_col[s]).astype(bf16)

    def norm_frame(j, c):
        norm0[j, c] = normed(window[j, c].astype(f32), 0)

    def own_norms(c, carry):
        take(c).wait()
        norm_frame(2 + y_lo, c)
        return carry

    lax.fori_loop(0, chunks, own_norms, 0)
    pl.when(early)(cross)

    first_plan = {0: (0, 1, 2), 1: (3, 4), 2: range(5, direct)}
    later_plan = {2: (0, 1, 2), 3: (3, 4, 5)}

    def arrive(c, carry):
        swap_in(c).wait_recv()
        at_left(lambda: deep_left(1, c).start())
        at_right(lambda: deep_right(1, c).start())
        norm_frame(3 - y_lo, c)
        for at in range(chunks):

            @pl.when(jnp.logical_and(early, c == at))
            def _():
                for i in first_plan.get(at, ()):
                    first_cut(i)
                if at == 2:
                    for i in shares:
                        first_side(i)

        pl.when(jnp.logical_and(patient, c == 2))(cross)
        at_left(lambda: deep_right(0, c).wait_recv())
        norm_frame(y_lo, c)
        at_right(lambda: deep_left(0, c).wait_recv())
        norm_frame(4 + y_lo, c)
        for at in range(chunks):

            @pl.when(jnp.logical_and(source, c == at))
            def _():
                for i in later_plan.get(at, ()):
                    forward_cut(i)

        @pl.when(jnp.logical_and(second, c == chunks - 1))
        def _():
            cross()
            for i in shares:
                forward_cut(i)

        return carry

    lax.fori_loop(0, chunks, arrive, 0)
    pass_film()
    pl.when(y_hi == 1)(lambda: own_to_sibling(seg).start())
    for load in loads[5:7]:
        load.wait()
    for n in range(2):
        for k in range(C // LANES + 1):
            lo, hi = k * LANES, min((k + 1) * LANES, C)
            skt[n, :, lo:hi] = raw_skip[n * C + lo : n * C + hi, :].T


    def await_section(s):
        @pl.when(sib_own == s)
        def _():
            own_to_sibling(sib_own).wait_recv()
            film_copy(sib_own, 0, sibling).wait_recv()

        @pl.when(relayed == s)
        def _():
            for q in range(pieces):
                to_sibling(relayed, q).wait_recv()
            film_copy(relayed, 2, sibling).wait_recv()

        modulate(s)

    def section(s, normals, base, skip=None, parts=1):
        count = len(normals) - 2
        pad = jnp.zeros((4 * C - 3 * C - 2 * LANES, count * LANES), bf16)
        taps = [jnp.concatenate(normals[t : t + count], axis=1) for t in range(3)]
        stacked = jnp.concatenate(taps + [pad], axis=0)
        hidden = []
        for part in range(parts):
            rows = slice(part * C // parts, (part + 1) * C // parts)
            mixed = jnp.dot(wt[s, rows, : 8 * LANES], stacked, preferred_element_type=f32)
            scale = jnp.concatenate([film_col[s, rows]] * count, axis=1)
            hidden.append(jax.nn.silu(mixed * scale).astype(bf16))
        weights = wt[s, :, 7 * LANES :]
        fields = [pad] + hidden
        if skip is not None:
            weights = jnp.concatenate([weights, skt[s - 2]], axis=1)
            fields = fields + [skip]
        total = base.astype(f32) + jnp.dot(weights, jnp.concatenate(fields, axis=0), preferred_element_type=f32)
        return total.astype(bf16)

    def to_left(s, c):
        return remote(
            nrm.at[s - 2, 0, c], halo_r.at[s - 2, c], halo_send.at[0, s - 2, c], halo_recv.at[1, s - 2, c], left
        )

    def to_right(s, c):
        return remote(
            nrm.at[s - 2, 1, c], halo_l.at[s - 2, c], halo_send.at[1, s - 2, c], halo_recv.at[0, s - 2, c], right
        )

    def keep(result, s, c):
        state[s - 1, 0, c] = result[:, :LANES]
        state[s - 1, 1, c] = result[:, LANES:]
        values = result.astype(f32)
        nrm[s - 2, 0, c] = normed(values[:, :LANES], s)
        at_left(lambda: to_left(s, c).start())
        nrm[s - 2, 1, c] = normed(values[:, LANES:], s)
        at_right(lambda: to_right(s, c).start())

    def frames_of(ref, j, c):
        return jnp.concatenate([ref[j, c], ref[j + 1, c]], axis=1)

    await_section(0)

    def deep_step(c, carry):
        at_left(lambda: deep_right(1, c).wait_recv())
        norm_frame(1 - y_lo, c)
        at_right(lambda: deep_left(1, c).wait_recv())
        norm_frame(5 - y_lo, c)
        base = jnp.concatenate([window[j, c] for j in range(1, 5)], axis=1)
        wide = section(0, [norm0[j, c] for j in range(6)], base)
        state[0, 0, c] = wide[:, LANES : 2 * LANES]
        state[0, 1, c] = wide[:, 2 * LANES : 3 * LANES]
        values = wide.astype(f32)
        nothing = jnp.zeros((C, LANES), bf16)
        norm1[0] = jnp.where(has_left, normed(values[:, :LANES], 1), nothing)
        norm1[1] = normed(values[:, LANES : 2 * LANES], 1)
        norm1[2] = normed(values[:, 2 * LANES : 3 * LANES], 1)
        norm1[3] = jnp.where(has_right, normed(values[:, 3 * LANES :], 1), nothing)

        @pl.when(c == 0)
        def _():
            @pl.when(second)
            def _():
                for i in range(SHARED, direct):
                    forward_cut(i)
                for i in shares:
                    forward_side(i)

            await_section(1)

        keep(section(1, [norm1[j] for j in range(4)], frames_of(state.at[0], 0, c), parts=2), 2, c)
        @pl.when(jnp.logical_and(source, c == 0))
        def _():
            for i in range(6, direct):
                forward_cut(i)

        @pl.when(jnp.logical_and(source, c == 1))
        def _():
            for i in shares:
                forward_side(i)

        return carry

    lax.fori_loop(0, chunks, deep_step, 0)

    def back_out(c):
        return remote(
            give.at[c], out_ref.at[0, 0, :, pixels(y_lo, c)], back_send.at[c], back_recv.at[c], partner
        )

    def back_in(c):
        return remote(
            give.at[c], out_ref.at[0, 0, :, pixels(1 - y_lo, c)], back_send.at[c], back_recv.at[c], partner
        )

    for s in (2, 3):
        await_section(s)

        def step(c, carry):
            at_left(lambda: to_right(s, c).wait_recv())
            at_right(lambda: to_left(s, c).wait_recv())
            normals = [halo_l[s - 2, c], nrm[s - 2, 0, c], nrm[s - 2, 1, c], halo_r[s - 2, c]]
            skip = frames_of(state.at[0], 0, c) if s == 2 else frames_of(window, 2, c)
            result = section(s, normals, frames_of(state.at[s - 1], 0, c), skip, parts=2)
            if s == 2:
                keep(result, 3, c)

                @pl.when(jnp.logical_and(patient, c == 0))
                def _():
                    for i in shares:
                        forward_cut(i)

                @pl.when(jnp.logical_and(patient, c == 1))
                def _():
                    for i in range(SHARED, direct):
                        forward_cut(i)

                @pl.when(jnp.logical_and(patient, c == 2))
                def _():
                    for i in shares:
                        forward_side(i)

            else:
                give[c] = jnp.where(y_lo == 0, result[:, LANES:], result[:, :LANES])
                back_out(c).start()
                out_ref[0, 0, :, pixels(y_lo, c)] = jnp.where(y_lo == 0, result[:, :LANES], result[:, LANES:])
            return carry

        lax.fori_loop(0, chunks, step, 0)

    def finish(c, carry):
        swap(c).wait_send()
        for kind in range(2):
            at_left(lambda: deep_left(kind, c).wait_send())
            at_right(lambda: deep_right(kind, c).wait_send())
        for s in (2, 3):
            at_left(lambda: to_left(s, c).wait_send())
            at_right(lambda: to_right(s, c).wait_send())
        return carry

    lax.fori_loop(0, chunks, finish, 0)
    own_to_sibling(seg).wait_send()
    @pl.when(source)
    def _():
        for i in range(direct):
            to_across(seg, order(x_par, i)).wait_send()

    @pl.when(jnp.logical_not(source))
    def _():
        for i in range(direct):
            to_across(seg, order(1 - y_lo, i)).wait_send()

    @pl.when(early)
    def _():
        for i in shares:
            to_ahead(gathered, order(x_par, i)).wait_send()

    @pl.when(jnp.logical_not(early))
    def _():
        for i in shares:
            to_partner(gathered, order(y_lo, i)).wait_send()

    for q in range(pieces):
        to_sibling(gathered, q).wait_send()
    film_copy(seg, 0, sibling).wait_send()
    film_copy(seg, 1, across).wait_send()
    film_copy(gathered, 2, sibling).wait_send()

    def returned(c, carry):
        back_out(c).wait_send()
        back_in(c).wait_recv()
        return carry

    lax.fori_loop(0, chunks, returned, 0)


def shards(geometry, clips, timesteps, gain, temporal_weight, film_weight, out_weight, skip_weight):
    C, chunks, frames = geometry
    pieces = 4 * C // LANES
    base = np.exp(-math.log(10000.0) * np.arange(C // 2) / (C // 2))
    freq = jnp.asarray(np.concatenate([base, base])[None, :].astype(np.float32))
    hbm = pl.BlockSpec(memory_space=pltpu.HBM)
    bf16, f32 = jnp.bfloat16, jnp.float32
    dma = pltpu.SemaphoreType.DMA
    flops = 2 * 22 * C * C * 2 * chunks * LANES
    return pl.pallas_call(
        functools.partial(unet_kernel, geometry),
        out_shape=pltpu.VMEM(clips.shape, bf16),
        in_specs=[hbm] * 8,
        out_specs=pl.BlockSpec(memory_space=pltpu.VMEM),
        scratch_shapes=[
            pltpu.SMEM(timesteps.shape, jnp.int32),
            pltpu.VMEM(freq.shape, f32),
            pltpu.VMEM(gain.shape, f32),
            pltpu.VMEM((4 * C, C), bf16),
            pltpu.VMEM((2 * C, C), bf16),
            pltpu.VMEM((C, C), bf16),
            pltpu.VMEM((SECTIONS, C, 4 * C), bf16),
            pltpu.VMEM((2, C, C), bf16),
            pltpu.VMEM((SECTIONS, EMB_ROWS, C), f32),
            pltpu.VMEM((SECTIONS, C, LANES), f32),
            pltpu.VMEM((SECTIONS, C, LANES), f32),
            pltpu.VMEM((6, chunks, C, LANES), bf16),
            pltpu.VMEM((6, chunks, C, LANES), bf16),
            pltpu.VMEM((4, C, LANES), bf16),
            pltpu.VMEM((3, 2, chunks, C, LANES), bf16),
            pltpu.VMEM((2, 2, chunks, C, LANES), bf16),
            pltpu.VMEM((2, chunks, C, LANES), bf16),
            pltpu.VMEM((2, chunks, C, LANES), bf16),
            pltpu.VMEM((chunks, C, LANES), bf16),
            dma((10,)),
            dma((chunks,)),
            dma((chunks,)),
            dma((chunks,)),
            dma((2, 2, chunks)),
            dma((2, 2, chunks)),
            dma((2, 2, chunks)),
            dma((2, 2, chunks)),
            dma((1,)),
            dma((1,)),
            dma((pieces,)),
            dma((pieces,)),
            dma((pieces,)),
            dma((pieces,)),
            dma((pieces,)),
            dma((pieces,)),
            dma((3,)),
            dma((3,)),
            dma((chunks,)),
            dma((chunks,)),
        ],
        compiler_params=pltpu.CompilerParams(
            collective_id=0, has_side_effects=True, vmem_limit_bytes=60 * 10**6
        ),
        cost_estimate=pl.CostEstimate(flops=flops, bytes_accessed=4 * clips.size, transcendentals=0),
        name="unet",
    )(timesteps, freq, gain, temporal_weight, film_weight, out_weight, skip_weight, clips)


def solution(mesh):
    frames = mesh.shape["frame"]

    def run(clips, *rest):
        _, _, C, pix = clips.shape
        geometry = (C, pix // 2 // LANES, frames)
        return shards(geometry, clips, *rest)

    placed = (
        P("segment", "frame", None, None),
        P(),
        P(),
        P("segment", None, None, None),
        P("segment", None, None),
        P("segment", None, None),
        P(),
    )
    return jax.shard_map(
        run,
        mesh=mesh,
        in_specs=placed,
        out_specs=P("segment", "frame", None, None),
        check_vma=False,
    )
```

```python
import functools
import math

import jax
import jax.numpy as jnp
import numpy as np
from jax import lax
from jax.experimental import pallas as pl
from jax.experimental.pallas import tpu as pltpu
from jax.sharding import PartitionSpec as P

MESH = pl.DeviceIdType.MESH
LANES = 128
SECTIONS = 4
EMB_ROWS = 8
SHARED = 4


def unet_kernel(
    geometry,
    time_ref,
    freq_ref,
    gain_ref,
    taps_ref,
    film_ref,
    proj_ref,
    skip_ref,
    clips_ref,
    out_ref,
    time_smem,
    freq_vmem,
    gain_vmem,
    raw,
    raw_skip,
    raw_film,
    wt,
    skt,
    film_rows,
    film_col,
    gain_col,
    window,
    norm0,
    norm1,
    state,
    nrm,
    halo_l,
    halo_r,
    give,
    load_sem,
    take_sem,
    swap_send,
    swap_recv,
    deep_send,
    deep_recv,
    halo_send,
    halo_recv,
    own_send,
    own_recv,
    cut_send,
    cut_recv,
    side_send,
    side_recv,
    sib_send,
    sib_recv,
    film_send,
    film_recv,
    back_send,
    back_recv,
):
    C, chunks, frames = geometry
    pieces = 4 * C // LANES
    direct = pieces - SHARED
    half_pix = chunks * LANES
    groups = frames // 2
    f32, bf16 = jnp.float32, jnp.bfloat16

    seg = lax.axis_index("segment")
    frame = lax.axis_index("frame")
    y_hi, core = seg // 2, seg % 2
    group, y_lo = frame // 2, frame % 2

    partner = (seg, group * 2 + 1 - y_lo)
    left = (seg, frame - 2)
    right = (seg, frame + 2)
    sibling = (y_hi * 2 + 1 - core, frame)
    across = ((1 - y_hi) * 2 + core, group * 2 + 1 - y_lo)
    x_step = 16 if frames >= 32 else 2
    spread = frames // x_step
    x_par = (frame // x_step) % 2
    turn_x = jnp.where((frame % x_step) // 2 == x_step // 2 - 1, 1, spread - 1)
    ahead = (seg, (frame + x_step * turn_x) % frames)
    behind = (seg, (frame + x_step * (spread - turn_x)) % frames)
    has_left = group > 0
    has_right = group < groups - 1
    gathered = (1 - y_hi) * 2 + core
    relayed = (1 - y_hi) * 2 + 1 - core
    sib_own = y_hi * 2 + 1 - core
    early = jnp.logical_and(y_hi == 1, core == 0)
    second = jnp.logical_and(y_hi == 1, core == 1)
    patient = jnp.logical_and(y_hi == 0, core == 1)

    def remote(src, dst, send, recv, device):
        return pltpu.make_async_remote_copy(
            src_ref=src, dst_ref=dst, send_sem=send, recv_sem=recv, device_id=device, device_id_type=MESH
        )

    def at_left(action):
        pl.when(has_left)(action)

    def at_right(action):
        pl.when(has_right)(action)

    loads = [
        pltpu.make_async_copy(taps_ref.at[0, 0], raw.at[pl.ds(0, C)], load_sem.at[0]),
        pltpu.make_async_copy(taps_ref.at[0, 1], raw.at[pl.ds(C, C)], load_sem.at[1]),
        pltpu.make_async_copy(taps_ref.at[0, 2], raw.at[pl.ds(2 * C, C)], load_sem.at[2]),
        pltpu.make_async_copy(proj_ref.at[0], raw.at[pl.ds(3 * C, C)], load_sem.at[3]),
        pltpu.make_async_copy(film_ref.at[0], raw_film, load_sem.at[4]),
        pltpu.make_async_copy(skip_ref.at[0], raw_skip.at[pl.ds(0, C)], load_sem.at[5]),
        pltpu.make_async_copy(skip_ref.at[1], raw_skip.at[pl.ds(C, C)], load_sem.at[6]),
        pltpu.make_async_copy(time_ref, time_smem, load_sem.at[7]),
        pltpu.make_async_copy(freq_ref, freq_vmem, load_sem.at[8]),
        pltpu.make_async_copy(gain_ref, gain_vmem, load_sem.at[9]),
    ]
    for load in loads[:4]:
        load.start()

    def pixels(part, c):
        return pl.ds(pl.multiple_of(part * half_pix + c * LANES, LANES), LANES)

    def take(c):
        return pltpu.make_async_copy(
            clips_ref.at[0, 0, :, pixels(y_lo, c)], window.at[2 + y_lo, c], take_sem.at[c]
        )

    for c in range(chunks):
        take(c).start()
    for load in loads[4:]:
        load.start()

    barrier = pltpu.get_barrier_semaphore()
    at_left(lambda: pl.semaphore_signal(barrier, inc=1, device_id=left, device_id_type=MESH))
    at_right(lambda: pl.semaphore_signal(barrier, inc=1, device_id=right, device_id_type=MESH))
    for device in (partner, sibling, across):
        pl.semaphore_signal(barrier, inc=1, device_id=device, device_id_type=MESH)

    @pl.when(early)
    def _():
        for device in (ahead, behind):
            pl.semaphore_signal(barrier, inc=1, device_id=device, device_id_type=MESH)

    def turn():
        for load in loads[:4]:
            load.wait()
        for k in range(pieces):
            wt[seg, :, k * LANES : (k + 1) * LANES] = raw[k * LANES : (k + 1) * LANES, :].T

    source = jnp.logical_and(y_hi == 0, core == 0)
    pl.when(source)(turn)

    pl.semaphore_wait(barrier, 3 + 2 * early.astype(jnp.int32) + has_left.astype(jnp.int32) + has_right.astype(jnp.int32))

    def swap(c):
        return remote(
            clips_ref.at[0, 0, :, pixels(1 - y_lo, c)],
            window.at[2 + y_lo, c],
            swap_send.at[c],
            swap_recv.at[c],
            partner,
        )

    def swap_in(c):
        return remote(
            clips_ref.at[0, 0, :, pixels(y_lo, c)],
            window.at[3 - y_lo, c],
            swap_send.at[c],
            swap_recv.at[c],
            partner,
        )

    def deep_left(kind, c):
        which = y_lo if kind == 0 else 1 - y_lo
        return remote(
            clips_ref.at[0, 0, :, pixels(y_lo, c)] if kind == 0 else window.at[2 + which, c], window.at[4 + which, c], deep_send.at[0, kind, c], deep_recv.at[0, kind, c], left
        )

    def deep_right(kind, c):
        which = y_lo if kind == 0 else 1 - y_lo
        return remote(
            clips_ref.at[0, 0, :, pixels(y_lo, c)] if kind == 0 else window.at[2 + which, c], window.at[which, c], deep_send.at[1, kind, c], deep_recv.at[1, kind, c], right
        )

    def block(index, q):
        return wt.at[index, :, pl.ds(pl.multiple_of(q * LANES, LANES), LANES)]

    def own_to_sibling(index):
        return remote(wt.at[index], wt.at[index], own_send.at[0], own_recv.at[0], sibling)

    def to_across(index, q):
        return remote(block(index, q), block(index, q), cut_send.at[q], cut_recv.at[q], across)

    def to_partner(index, q):
        return remote(block(index, q), block(index, q), side_send.at[q], side_recv.at[q], partner)

    def to_sibling(index, q):
        return remote(block(index, q), block(index, q), sib_send.at[q], sib_recv.at[q], sibling)

    def to_ahead(index, q):
        return remote(block(index, q), block(index, q), side_send.at[q], side_recv.at[q], ahead)

    def order(parity, i):
        return i + parity * (pieces - 1 - 2 * i)

    def first_cut(i):
        q = order(x_par, i)
        to_across(gathered, q).wait_recv()
        if i < SHARED:
            to_ahead(gathered, q).start()
        to_sibling(gathered, q).start()

    def first_side(i):
        q = order(1 - x_par, i)
        to_ahead(gathered, q).wait_recv()
        to_sibling(gathered, q).start()

    def forward_cut(i):
        q = order(y_lo, i)
        to_across(gathered, q).wait_recv()
        if i < SHARED:
            to_partner(gathered, q).start()
        to_sibling(gathered, q).start()

    def forward_side(i):
        q = order(1 - y_lo, i)
        to_partner(gathered, q).wait_recv()
        to_sibling(gathered, q).start()

    def cross_first():
        for i in range(direct):
            to_across(seg, order(x_par, i)).start()

    def cross():
        for i in range(direct):
            to_across(seg, order(1 - y_lo, i)).start()

    shares = range(SHARED)
    pl.when(source)(cross_first)

    for c in range(chunks):
        swap(c).start()
        at_left(lambda: deep_left(0, c).start())
        at_right(lambda: deep_right(0, c).start())

    pl.when(patient)(turn)
    pl.when(y_hi == 0)(lambda: own_to_sibling(seg).start())

    for load in loads[7:]:
        load.wait()
    row = lax.broadcasted_iota(jnp.int32, (EMB_ROWS, 1), 0)
    when = jnp.zeros((EMB_ROWS, 1), jnp.int32)
    for m in range(SECTIONS):
        when = jnp.where(row == m, time_smem[m], when)
    angle = when.astype(f32) * freq_vmem[...]
    lane = lax.broadcasted_iota(jnp.int32, angle.shape, 1)
    emb = jnp.where(lane < C // 2, jnp.sin(angle), jnp.cos(angle)).astype(bf16)
    loads[4].wait()
    film_rows[seg] = jnp.dot(emb, raw_film[...], preferred_element_type=f32)

    def film_copy(index, which, device):
        return remote(film_rows.at[index], film_rows.at[index], film_send.at[which], film_recv.at[which], device)

    film_copy(seg, 0, sibling).start()
    film_copy(seg, 1, across).start()

    def pass_film():
        film_copy(gathered, 1, across).wait_recv()
        film_copy(gathered, 2, sibling).start()

    def column(values):
        return jnp.broadcast_to(values, (LANES, C)).T

    def modulate(s):
        mine = jnp.sum(jnp.where(row == seg, film_rows[s], 0.0), axis=0, keepdims=True)
        film_col[s] = column(1.0 + mine)

    for s in range(SECTIONS):
        gain_col[s] = column(gain_vmem[s : s + 1, :])

    @pl.when(jnp.logical_not(has_left))
    def _():
        halo_l[...] = jnp.zeros_like(halo_l)
        window[0:2] = jnp.zeros((2, chunks, C, LANES), bf16)

    @pl.when(jnp.logical_not(has_right))
    def _():
        halo_r[...] = jnp.zeros_like(halo_r)
        window[4:6] = jnp.zeros((2, chunks, C, LANES), bf16)

    def normed(values, s):
        meansq = jnp.sum(values * values, axis=0, keepdims=True) * (1.0 / C)
        return (values * lax.rsqrt(meansq + 1e-05) * gain_col[s]).astype(bf16)

    def norm_frame(j, c):
        norm0[j, c] = normed(window[j, c].astype(f32), 0)

    def own_norms(c, carry):
        take(c).wait()
        norm_frame(2 + y_lo, c)
        return carry

    lax.fori_loop(0, chunks, own_norms, 0)
    pl.when(y_hi == 1)(turn)
    pl.when(early)(cross)

    first_plan = {0: (0, 1, 2), 1: (3, 4), 2: range(5, direct)}
    later_plan = {2: (0, 1, 2), 3: (3, 4, 5)}

    def arrive(c, carry):
        swap_in(c).wait_recv()
        at_left(lambda: deep_left(1, c).start())
        at_right(lambda: deep_right(1, c).start())
        norm_frame(3 - y_lo, c)
        for at in range(chunks):

            @pl.when(jnp.logical_and(early, c == at))
            def _():
                for i in first_plan.get(at, ()):
                    first_cut(i)
                if at == 2:
                    for i in shares:
                        first_side(i)

        pl.when(jnp.logical_and(patient, c == 2))(cross)
        at_left(lambda: deep_right(0, c).wait_recv())
        norm_frame(y_lo, c)
        at_right(lambda: deep_left(0, c).wait_recv())
        norm_frame(4 + y_lo, c)
        for at in range(chunks):

            @pl.when(jnp.logical_and(source, c == at))
            def _():
                for i in later_plan.get(at, ()):
                    forward_cut(i)

        @pl.when(jnp.logical_and(second, c == chunks - 1))
        def _():
            cross()
            for i in shares:
                forward_cut(i)

        return carry

    lax.fori_loop(0, chunks, arrive, 0)
    pass_film()
    pl.when(y_hi == 1)(lambda: own_to_sibling(seg).start())
    for load in loads[5:7]:
        load.wait()
    for n in range(2):
        for k in range(C // LANES + 1):
            lo, hi = k * LANES, min((k + 1) * LANES, C)
            skt[n, :, lo:hi] = raw_skip[n * C + lo : n * C + hi, :].T


    def await_section(s):
        @pl.when(sib_own == s)
        def _():
            own_to_sibling(sib_own).wait_recv()
            film_copy(sib_own, 0, sibling).wait_recv()

        @pl.when(relayed == s)
        def _():
            for q in range(pieces):
                to_sibling(relayed, q).wait_recv()
            film_copy(relayed, 2, sibling).wait_recv()

        modulate(s)

    def section(s, normals, base, skip=None, parts=1):
        count = len(normals) - 2
        pad = jnp.zeros((4 * C - 3 * C - 2 * LANES, count * LANES), bf16)
        taps = [jnp.concatenate(normals[t : t + count], axis=1) for t in range(3)]
        stacked = jnp.concatenate(taps + [pad], axis=0)
        hidden = []
        for part in range(parts):
            rows = slice(part * C // parts, (part + 1) * C // parts)
            mixed = jnp.dot(wt[s, rows, : 8 * LANES], stacked, preferred_element_type=f32)
            scale = jnp.concatenate([film_col[s, rows]] * count, axis=1)
            hidden.append(jax.nn.silu(mixed * scale).astype(bf16))
        weights = wt[s, :, 7 * LANES :]
        fields = [pad] + hidden
        if skip is not None:
            weights = jnp.concatenate([weights, skt[s - 2]], axis=1)
            fields = fields + [skip]
        total = base.astype(f32) + jnp.dot(weights, jnp.concatenate(fields, axis=0), preferred_element_type=f32)
        return total.astype(bf16)

    def to_left(s, c):
        return remote(
            nrm.at[s - 2, 0, c], halo_r.at[s - 2, c], halo_send.at[0, s - 2, c], halo_recv.at[1, s - 2, c], left
        )

    def to_right(s, c):
        return remote(
            nrm.at[s - 2, 1, c], halo_l.at[s - 2, c], halo_send.at[1, s - 2, c], halo_recv.at[0, s - 2, c], right
        )

    def keep(result, s, c):
        state[s - 1, 0, c] = result[:, :LANES]
        state[s - 1, 1, c] = result[:, LANES:]
        values = result.astype(f32)
        nrm[s - 2, 0, c] = normed(values[:, :LANES], s)
        at_left(lambda: to_left(s, c).start())
        nrm[s - 2, 1, c] = normed(values[:, LANES:], s)
        at_right(lambda: to_right(s, c).start())

    def frames_of(ref, j, c):
        return jnp.concatenate([ref[j, c], ref[j + 1, c]], axis=1)

    await_section(0)

    def deep_step(c, carry):
        at_left(lambda: deep_right(1, c).wait_recv())
        norm_frame(1 - y_lo, c)
        at_right(lambda: deep_left(1, c).wait_recv())
        norm_frame(5 - y_lo, c)
        base = jnp.concatenate([window[j, c] for j in range(1, 5)], axis=1)
        wide = section(0, [norm0[j, c] for j in range(6)], base)
        state[0, 0, c] = wide[:, LANES : 2 * LANES]
        state[0, 1, c] = wide[:, 2 * LANES : 3 * LANES]
        values = wide.astype(f32)
        nothing = jnp.zeros((C, LANES), bf16)
        norm1[0] = jnp.where(has_left, normed(values[:, :LANES], 1), nothing)
        norm1[1] = normed(values[:, LANES : 2 * LANES], 1)
        norm1[2] = normed(values[:, 2 * LANES : 3 * LANES], 1)
        norm1[3] = jnp.where(has_right, normed(values[:, 3 * LANES :], 1), nothing)

        @pl.when(c == 0)
        def _():
            @pl.when(second)
            def _():
                for i in range(SHARED, direct):
                    forward_cut(i)
                for i in shares:
                    forward_side(i)

            await_section(1)

        keep(section(1, [norm1[j] for j in range(4)], frames_of(state.at[0], 0, c), parts=2), 2, c)
        @pl.when(jnp.logical_and(source, c == 0))
        def _():
            for i in range(6, direct):
                forward_cut(i)

        @pl.when(jnp.logical_and(source, c == 1))
        def _():
            for i in shares:
                forward_side(i)

        return carry

    lax.fori_loop(0, chunks, deep_step, 0)

    def back_out(c):
        return remote(
            give.at[c], out_ref.at[0, 0, :, pixels(y_lo, c)], back_send.at[c], back_recv.at[c], partner
        )

    def back_in(c):
        return remote(
            give.at[c], out_ref.at[0, 0, :, pixels(1 - y_lo, c)], back_send.at[c], back_recv.at[c], partner
        )

    for s in (2, 3):
        await_section(s)

        def step(c, carry):
            at_left(lambda: to_right(s, c).wait_recv())
            at_right(lambda: to_left(s, c).wait_recv())
            normals = [halo_l[s - 2, c], nrm[s - 2, 0, c], nrm[s - 2, 1, c], halo_r[s - 2, c]]
            skip = frames_of(state.at[0], 0, c) if s == 2 else frames_of(window, 2, c)
            result = section(s, normals, frames_of(state.at[s - 1], 0, c), skip, parts=2)
            if s == 2:
                keep(result, 3, c)

                @pl.when(jnp.logical_and(patient, c == 0))
                def _():
                    for i in shares:
                        forward_cut(i)

                @pl.when(jnp.logical_and(patient, c == 1))
                def _():
                    for i in range(SHARED, direct):
                        forward_cut(i)

                @pl.when(jnp.logical_and(patient, c == 2))
                def _():
                    for i in shares:
                        forward_side(i)

            else:
                give[c] = jnp.where(y_lo == 0, result[:, LANES:], result[:, :LANES])
                back_out(c).start()
                out_ref[0, 0, :, pixels(y_lo, c)] = jnp.where(y_lo == 0, result[:, :LANES], result[:, LANES:])
            return carry

        lax.fori_loop(0, chunks, step, 0)

    def finish(c, carry):
        swap(c).wait_send()
        for kind in range(2):
            at_left(lambda: deep_left(kind, c).wait_send())
            at_right(lambda: deep_right(kind, c).wait_send())
        for s in (2, 3):
            at_left(lambda: to_left(s, c).wait_send())
            at_right(lambda: to_right(s, c).wait_send())
        return carry

    lax.fori_loop(0, chunks, finish, 0)
    own_to_sibling(seg).wait_send()
    @pl.when(source)
    def _():
        for i in range(direct):
            to_across(seg, order(x_par, i)).wait_send()

    @pl.when(jnp.logical_not(source))
    def _():
        for i in range(direct):
            to_across(seg, order(1 - y_lo, i)).wait_send()

    @pl.when(early)
    def _():
        for i in shares:
            to_ahead(gathered, order(x_par, i)).wait_send()

    @pl.when(jnp.logical_not(early))
    def _():
        for i in shares:
            to_partner(gathered, order(y_lo, i)).wait_send()

    for q in range(pieces):
        to_sibling(gathered, q).wait_send()
    film_copy(seg, 0, sibling).wait_send()
    film_copy(seg, 1, across).wait_send()
    film_copy(gathered, 2, sibling).wait_send()

    def returned(c, carry):
        back_out(c).wait_send()
        back_in(c).wait_recv()
        return carry

    lax.fori_loop(0, chunks, returned, 0)


def shards(geometry, clips, timesteps, gain, temporal_weight, film_weight, out_weight, skip_weight):
    C, chunks, frames = geometry
    pieces = 4 * C // LANES
    base = np.exp(-math.log(10000.0) * np.arange(C // 2) / (C // 2))
    freq = jnp.asarray(np.concatenate([base, base])[None, :].astype(np.float32))
    hbm = pl.BlockSpec(memory_space=pltpu.HBM)
    bf16, f32 = jnp.bfloat16, jnp.float32
    dma = pltpu.SemaphoreType.DMA
    flops = 2 * 22 * C * C * 2 * chunks * LANES
    return pl.pallas_call(
        functools.partial(unet_kernel, geometry),
        out_shape=pltpu.VMEM(clips.shape, bf16),
        in_specs=[hbm] * 8,
        out_specs=pl.BlockSpec(memory_space=pltpu.VMEM),
        scratch_shapes=[
            pltpu.SMEM(timesteps.shape, jnp.int32),
            pltpu.VMEM(freq.shape, f32),
            pltpu.VMEM(gain.shape, f32),
            pltpu.VMEM((4 * C, C), bf16),
            pltpu.VMEM((2 * C, C), bf16),
            pltpu.VMEM((C, C), bf16),
            pltpu.VMEM((SECTIONS, C, 4 * C), bf16),
            pltpu.VMEM((2, C, C), bf16),
            pltpu.VMEM((SECTIONS, EMB_ROWS, C), f32),
            pltpu.VMEM((SECTIONS, C, LANES), f32),
            pltpu.VMEM((SECTIONS, C, LANES), f32),
            pltpu.VMEM((6, chunks, C, LANES), bf16),
            pltpu.VMEM((6, chunks, C, LANES), bf16),
            pltpu.VMEM((4, C, LANES), bf16),
            pltpu.VMEM((3, 2, chunks, C, LANES), bf16),
            pltpu.VMEM((2, 2, chunks, C, LANES), bf16),
            pltpu.VMEM((2, chunks, C, LANES), bf16),
            pltpu.VMEM((2, chunks, C, LANES), bf16),
            pltpu.VMEM((chunks, C, LANES), bf16),
            dma((10,)),
            dma((chunks,)),
            dma((chunks,)),
            dma((chunks,)),
            dma((2, 2, chunks)),
            dma((2, 2, chunks)),
            dma((2, 2, chunks)),
            dma((2, 2, chunks)),
            dma((1,)),
            dma((1,)),
            dma((pieces,)),
            dma((pieces,)),
            dma((pieces,)),
            dma((pieces,)),
            dma((pieces,)),
            dma((pieces,)),
            dma((3,)),
            dma((3,)),
            dma((chunks,)),
            dma((chunks,)),
        ],
        compiler_params=pltpu.CompilerParams(
            collective_id=0, has_side_effects=True, vmem_limit_bytes=60 * 10**6
        ),
        cost_estimate=pl.CostEstimate(flops=flops, bytes_accessed=4 * clips.size, transcendentals=0),
        name="unet",
    )(timesteps, freq, gain, temporal_weight, film_weight, out_weight, skip_weight, clips)


def solution(mesh):
    frames = mesh.shape["frame"]

    def run(clips, *rest):
        _, _, C, pix = clips.shape
        geometry = (C, pix // 2 // LANES, frames)
        return shards(geometry, clips, *rest)

    placed = (
        P("segment", "frame", None, None),
        P(),
        P(),
        P("segment", None, None, None),
        P("segment", None, None),
        P("segment", None, None),
        P(),
    )
    return jax.shard_map(
        run,
        mesh=mesh,
        in_specs=placed,
        out_specs=P("segment", "frame", None, None),
        check_vma=False,
    )
```

```python
import functools
import math

import jax
import jax.numpy as jnp
import numpy as np
from jax import lax
from jax.experimental import pallas as pl
from jax.experimental.pallas import tpu as pltpu
from jax.sharding import PartitionSpec as P

MESH = pl.DeviceIdType.MESH
LANES = 128
SECTIONS = 4
EMB_ROWS = 8
SHARED = 4


def unet_kernel(
    geometry,
    time_ref,
    freq_ref,
    gain_ref,
    taps_ref,
    film_ref,
    proj_ref,
    skip_ref,
    clips_ref,
    out_ref,
    time_smem,
    freq_vmem,
    gain_vmem,
    raw,
    raw_skip,
    raw_film,
    wt,
    skt,
    film_rows,
    film_col,
    gain_col,
    window,
    norm0,
    norm1,
    state,
    nrm,
    halo_l,
    halo_r,
    give,
    load_sem,
    take_sem,
    swap_send,
    swap_recv,
    deep_send,
    deep_recv,
    halo_send,
    halo_recv,
    own_send,
    own_recv,
    cut_send,
    cut_recv,
    side_send,
    side_recv,
    sib_send,
    sib_recv,
    film_send,
    film_recv,
    back_send,
    back_recv,
):
    C, chunks, frames = geometry
    pieces = 4 * C // LANES
    direct = pieces - SHARED
    half_pix = chunks * LANES
    groups = frames // 2
    f32, bf16 = jnp.float32, jnp.bfloat16

    seg = lax.axis_index("segment")
    frame = lax.axis_index("frame")
    y_hi, core = seg // 2, seg % 2
    group, y_lo = frame // 2, frame % 2

    partner = (seg, group * 2 + 1 - y_lo)
    left = (seg, frame - 2)
    right = (seg, frame + 2)
    sibling = (y_hi * 2 + 1 - core, frame)
    across = ((1 - y_hi) * 2 + core, group * 2 + 1 - y_lo)
    x_step = 16 if frames >= 32 else 2
    spread = frames // x_step
    x_par = (frame // x_step) % 2
    turn_x = jnp.where((frame % x_step) // 2 == x_step // 2 - 1, 1, spread - 1)
    ahead = (seg, (frame + x_step * turn_x) % frames)
    behind = (seg, (frame + x_step * (spread - turn_x)) % frames)
    has_left = group > 0
    has_right = group < groups - 1
    gathered = (1 - y_hi) * 2 + core
    relayed = (1 - y_hi) * 2 + 1 - core
    sib_own = y_hi * 2 + 1 - core
    early = jnp.logical_and(y_hi == 1, core == 0)
    second = jnp.logical_and(y_hi == 1, core == 1)
    patient = jnp.logical_and(y_hi == 0, core == 1)

    def remote(src, dst, send, recv, device):
        return pltpu.make_async_remote_copy(
            src_ref=src, dst_ref=dst, send_sem=send, recv_sem=recv, device_id=device, device_id_type=MESH
        )

    def at_left(action):
        pl.when(has_left)(action)

    def at_right(action):
        pl.when(has_right)(action)

    loads = [
        pltpu.make_async_copy(taps_ref.at[0, 0], raw.at[pl.ds(0, C)], load_sem.at[0]),
        pltpu.make_async_copy(taps_ref.at[0, 1], raw.at[pl.ds(C, C)], load_sem.at[1]),
        pltpu.make_async_copy(taps_ref.at[0, 2], raw.at[pl.ds(2 * C, C)], load_sem.at[2]),
        pltpu.make_async_copy(proj_ref.at[0], raw.at[pl.ds(3 * C, C)], load_sem.at[3]),
        pltpu.make_async_copy(film_ref.at[0], raw_film, load_sem.at[4]),
        pltpu.make_async_copy(skip_ref.at[0], raw_skip.at[pl.ds(0, C)], load_sem.at[5]),
        pltpu.make_async_copy(skip_ref.at[1], raw_skip.at[pl.ds(C, C)], load_sem.at[6]),
        pltpu.make_async_copy(time_ref, time_smem, load_sem.at[7]),
        pltpu.make_async_copy(freq_ref, freq_vmem, load_sem.at[8]),
        pltpu.make_async_copy(gain_ref, gain_vmem, load_sem.at[9]),
    ]
    for load in loads[:4]:
        load.start()

    def pixels(part, c):
        return pl.ds(pl.multiple_of(part * half_pix + c * LANES, LANES), LANES)

    def take(c):
        return pltpu.make_async_copy(
            clips_ref.at[0, 0, :, pixels(y_lo, c)], window.at[2 + y_lo, c], take_sem.at[c]
        )

    for c in range(chunks):
        take(c).start()
    for load in loads[4:]:
        load.start()

    barrier = pltpu.get_barrier_semaphore()
    at_left(lambda: pl.semaphore_signal(barrier, inc=1, device_id=left, device_id_type=MESH))
    at_right(lambda: pl.semaphore_signal(barrier, inc=1, device_id=right, device_id_type=MESH))
    for device in (partner, sibling, across):
        pl.semaphore_signal(barrier, inc=1, device_id=device, device_id_type=MESH)

    @pl.when(early)
    def _():
        for device in (ahead, behind):
            pl.semaphore_signal(barrier, inc=1, device_id=device, device_id_type=MESH)

    def turn():
        for load in loads[:4]:
            load.wait()
        for k in range(pieces):
            wt[seg, :, k * LANES : (k + 1) * LANES] = raw[k * LANES : (k + 1) * LANES, :].T

    source = jnp.logical_and(y_hi == 0, core == 0)
    pl.when(source)(turn)

    pl.semaphore_wait(barrier, 3 + 2 * early.astype(jnp.int32) + has_left.astype(jnp.int32) + has_right.astype(jnp.int32))

    def swap(c):
        return remote(
            clips_ref.at[0, 0, :, pixels(1 - y_lo, c)],
            window.at[2 + y_lo, c],
            swap_send.at[c],
            swap_recv.at[c],
            partner,
        )

    def swap_in(c):
        return remote(
            clips_ref.at[0, 0, :, pixels(y_lo, c)],
            window.at[3 - y_lo, c],
            swap_send.at[c],
            swap_recv.at[c],
            partner,
        )

    def deep_left(kind, c):
        which = y_lo if kind == 0 else 1 - y_lo
        return remote(
            clips_ref.at[0, 0, :, pixels(y_lo, c)] if kind == 0 else window.at[2 + which, c], window.at[4 + which, c], deep_send.at[0, kind, c], deep_recv.at[0, kind, c], left
        )

    def deep_right(kind, c):
        which = y_lo if kind == 0 else 1 - y_lo
        return remote(
            clips_ref.at[0, 0, :, pixels(y_lo, c)] if kind == 0 else window.at[2 + which, c], window.at[which, c], deep_send.at[1, kind, c], deep_recv.at[1, kind, c], right
        )

    def block(index, q):
        return wt.at[index, :, pl.ds(pl.multiple_of(q * LANES, LANES), LANES)]

    def own_to_sibling(index):
        return remote(wt.at[index], wt.at[index], own_send.at[0], own_recv.at[0], sibling)

    def to_across(index, q):
        return remote(block(index, q), block(index, q), cut_send.at[q], cut_recv.at[q], across)

    def to_partner(index, q):
        return remote(block(index, q), block(index, q), side_send.at[q], side_recv.at[q], partner)

    def to_sibling(index, q):
        return remote(block(index, q), block(index, q), sib_send.at[q], sib_recv.at[q], sibling)

    def to_ahead(index, q):
        return remote(block(index, q), block(index, q), side_send.at[q], side_recv.at[q], ahead)

    def order(parity, i):
        return i + parity * (pieces - 1 - 2 * i)

    def first_cut(i):
        q = order(x_par, i)
        to_across(gathered, q).wait_recv()
        if i < SHARED:
            to_ahead(gathered, q).start()
        to_sibling(gathered, q).start()

    def first_side(i):
        q = order(1 - x_par, i)
        to_ahead(gathered, q).wait_recv()
        to_sibling(gathered, q).start()

    def forward_cut(i):
        q = order(y_lo, i)
        to_across(gathered, q).wait_recv()
        if i < SHARED:
            to_partner(gathered, q).start()
        to_sibling(gathered, q).start()

    def forward_side(i):
        q = order(1 - y_lo, i)
        to_partner(gathered, q).wait_recv()
        to_sibling(gathered, q).start()

    def cross_first():
        for i in range(direct):
            to_across(seg, order(x_par, i)).start()

    def cross():
        for i in range(direct):
            to_across(seg, order(1 - y_lo, i)).start()

    shares = range(SHARED)
    pl.when(source)(cross_first)

    for c in range(chunks):
        swap(c).start()
        at_left(lambda: deep_left(0, c).start())
        at_right(lambda: deep_right(0, c).start())

    pl.when(source)(lambda: own_to_sibling(seg).start())

    for load in loads[7:]:
        load.wait()
    row = lax.broadcasted_iota(jnp.int32, (EMB_ROWS, 1), 0)
    when = jnp.zeros((EMB_ROWS, 1), jnp.int32)
    for m in range(SECTIONS):
        when = jnp.where(row == m, time_smem[m], when)
    angle = when.astype(f32) * freq_vmem[...]
    lane = lax.broadcasted_iota(jnp.int32, angle.shape, 1)
    emb = jnp.where(lane < C // 2, jnp.sin(angle), jnp.cos(angle)).astype(bf16)
    loads[4].wait()
    film_rows[seg] = jnp.dot(emb, raw_film[...], preferred_element_type=f32)

    def film_copy(index, which, device):
        return remote(film_rows.at[index], film_rows.at[index], film_send.at[which], film_recv.at[which], device)

    film_copy(seg, 0, sibling).start()
    film_copy(seg, 1, across).start()

    def pass_film():
        film_copy(gathered, 1, across).wait_recv()
        film_copy(gathered, 2, sibling).start()

    def column(values):
        return jnp.broadcast_to(values, (LANES, C)).T

    def modulate(s):
        mine = jnp.sum(jnp.where(row == seg, film_rows[s], 0.0), axis=0, keepdims=True)
        film_col[s] = column(1.0 + mine)

    for s in range(SECTIONS):
        gain_col[s] = column(gain_vmem[s : s + 1, :])

    @pl.when(jnp.logical_not(has_left))
    def _():
        halo_l[...] = jnp.zeros_like(halo_l)
        window[0:2] = jnp.zeros((2, chunks, C, LANES), bf16)

    @pl.when(jnp.logical_not(has_right))
    def _():
        halo_r[...] = jnp.zeros_like(halo_r)
        window[4:6] = jnp.zeros((2, chunks, C, LANES), bf16)

    def normed(values, s):
        meansq = jnp.sum(values * values, axis=0, keepdims=True) * (1.0 / C)
        return (values * lax.rsqrt(meansq + 1e-05) * gain_col[s]).astype(bf16)

    def norm_frame(j, c):
        norm0[j, c] = normed(window[j, c].astype(f32), 0)

    def own_norms(c, carry):
        take(c).wait()
        norm_frame(2 + y_lo, c)
        return carry

    lax.fori_loop(0, chunks, own_norms, 0)
    pl.when(jnp.logical_not(source))(turn)
    pl.when(patient)(lambda: own_to_sibling(seg).start())
    pl.when(early)(cross)

    first_plan = {0: (0, 1, 2), 1: (3, 4), 2: range(5, direct)}
    later_plan = {2: (0, 1, 2), 3: (3, 4, 5)}

    def arrive(c, carry):
        swap_in(c).wait_recv()
        at_left(lambda: deep_left(1, c).start())
        at_right(lambda: deep_right(1, c).start())
        norm_frame(3 - y_lo, c)
        for at in range(chunks):

            @pl.when(jnp.logical_and(early, c == at))
            def _():
                for i in first_plan.get(at, ()):
                    first_cut(i)
                if at == 2:
                    for i in shares:
                        first_side(i)

        pl.when(jnp.logical_and(patient, c == 2))(cross)
        at_left(lambda: deep_right(0, c).wait_recv())
        norm_frame(y_lo, c)
        at_right(lambda: deep_left(0, c).wait_recv())
        norm_frame(4 + y_lo, c)
        for at in range(chunks):

            @pl.when(jnp.logical_and(source, c == at))
            def _():
                for i in later_plan.get(at, ()):
                    forward_cut(i)

        @pl.when(jnp.logical_and(second, c == chunks - 1))
        def _():
            cross()
            for i in shares:
                forward_cut(i)

        return carry

    lax.fori_loop(0, chunks, arrive, 0)
    pass_film()
    pl.when(y_hi == 1)(lambda: own_to_sibling(seg).start())
    for load in loads[5:7]:
        load.wait()
    for n in range(2):
        for k in range(C // LANES + 1):
            lo, hi = k * LANES, min((k + 1) * LANES, C)
            skt[n, :, lo:hi] = raw_skip[n * C + lo : n * C + hi, :].T


    def await_section(s):
        @pl.when(sib_own == s)
        def _():
            own_to_sibling(sib_own).wait_recv()
            film_copy(sib_own, 0, sibling).wait_recv()

        @pl.when(relayed == s)
        def _():
            for q in range(pieces):
                to_sibling(relayed, q).wait_recv()
            film_copy(relayed, 2, sibling).wait_recv()

        modulate(s)

    def section(s, normals, base, skip=None, parts=1):
        count = len(normals) - 2
        pad = jnp.zeros((4 * C - 3 * C - 2 * LANES, count * LANES), bf16)
        taps = [jnp.concatenate(normals[t : t + count], axis=1) for t in range(3)]
        stacked = jnp.concatenate(taps + [pad], axis=0)
        hidden = []
        for part in range(parts):
            rows = slice(part * C // parts, (part + 1) * C // parts)
            mixed = jnp.dot(wt[s, rows, : 8 * LANES], stacked, preferred_element_type=f32)
            scale = jnp.concatenate([film_col[s, rows]] * count, axis=1)
            hidden.append(jax.nn.silu(mixed * scale).astype(bf16))
        weights = wt[s, :, 7 * LANES :]
        fields = [pad] + hidden
        if skip is not None:
            weights = jnp.concatenate([weights, skt[s - 2]], axis=1)
            fields = fields + [skip]
        total = base.astype(f32) + jnp.dot(weights, jnp.concatenate(fields, axis=0), preferred_element_type=f32)
        return total.astype(bf16)

    def to_left(s, c):
        return remote(
            nrm.at[s - 2, 0, c], halo_r.at[s - 2, c], halo_send.at[0, s - 2, c], halo_recv.at[1, s - 2, c], left
        )

    def to_right(s, c):
        return remote(
            nrm.at[s - 2, 1, c], halo_l.at[s - 2, c], halo_send.at[1, s - 2, c], halo_recv.at[0, s - 2, c], right
        )

    def keep(result, s, c):
        state[s - 1, 0, c] = result[:, :LANES]
        state[s - 1, 1, c] = result[:, LANES:]
        values = result.astype(f32)
        nrm[s - 2, 0, c] = normed(values[:, :LANES], s)
        at_left(lambda: to_left(s, c).start())
        nrm[s - 2, 1, c] = normed(values[:, LANES:], s)
        at_right(lambda: to_right(s, c).start())

    def frames_of(ref, j, c):
        return jnp.concatenate([ref[j, c], ref[j + 1, c]], axis=1)

    await_section(0)

    def deep_step(c, carry):
        at_left(lambda: deep_right(1, c).wait_recv())
        norm_frame(1 - y_lo, c)
        at_right(lambda: deep_left(1, c).wait_recv())
        norm_frame(5 - y_lo, c)
        base = jnp.concatenate([window[j, c] for j in range(1, 5)], axis=1)
        wide = section(0, [norm0[j, c] for j in range(6)], base)
        state[0, 0, c] = wide[:, LANES : 2 * LANES]
        state[0, 1, c] = wide[:, 2 * LANES : 3 * LANES]
        values = wide.astype(f32)
        nothing = jnp.zeros((C, LANES), bf16)
        norm1[0] = jnp.where(has_left, normed(values[:, :LANES], 1), nothing)
        norm1[1] = normed(values[:, LANES : 2 * LANES], 1)
        norm1[2] = normed(values[:, 2 * LANES : 3 * LANES], 1)
        norm1[3] = jnp.where(has_right, normed(values[:, 3 * LANES :], 1), nothing)

        @pl.when(c == 0)
        def _():
            @pl.when(second)
            def _():
                for i in range(SHARED, direct):
                    forward_cut(i)
                for i in shares:
                    forward_side(i)

            await_section(1)

        keep(section(1, [norm1[j] for j in range(4)], frames_of(state.at[0], 0, c), parts=2), 2, c)
        @pl.when(jnp.logical_and(source, c == 0))
        def _():
            for i in range(6, direct):
                forward_cut(i)

        @pl.when(jnp.logical_and(source, c == 1))
        def _():
            for i in shares:
                forward_side(i)

        return carry

    lax.fori_loop(0, chunks, deep_step, 0)

    def back_out(c):
        return remote(
            give.at[c], out_ref.at[0, 0, :, pixels(y_lo, c)], back_send.at[c], back_recv.at[c], partner
        )

    def back_in(c):
        return remote(
            give.at[c], out_ref.at[0, 0, :, pixels(1 - y_lo, c)], back_send.at[c], back_recv.at[c], partner
        )

    for s in (2, 3):
        await_section(s)

        def step(c, carry):
            at_left(lambda: to_right(s, c).wait_recv())
            at_right(lambda: to_left(s, c).wait_recv())
            normals = [halo_l[s - 2, c], nrm[s - 2, 0, c], nrm[s - 2, 1, c], halo_r[s - 2, c]]
            skip = frames_of(state.at[0], 0, c) if s == 2 else frames_of(window, 2, c)
            result = section(s, normals, frames_of(state.at[s - 1], 0, c), skip, parts=2)
            if s == 2:
                keep(result, 3, c)

                @pl.when(jnp.logical_and(patient, c == 0))
                def _():
                    for i in shares:
                        forward_cut(i)

                @pl.when(jnp.logical_and(patient, c == 1))
                def _():
                    for i in range(SHARED, direct):
                        forward_cut(i)

                @pl.when(jnp.logical_and(patient, c == 2))
                def _():
                    for i in shares:
                        forward_side(i)

            else:
                give[c] = jnp.where(y_lo == 0, result[:, LANES:], result[:, :LANES])
                back_out(c).start()
                out_ref[0, 0, :, pixels(y_lo, c)] = jnp.where(y_lo == 0, result[:, :LANES], result[:, LANES:])
            return carry

        lax.fori_loop(0, chunks, step, 0)

    def finish(c, carry):
        swap(c).wait_send()
        for kind in range(2):
            at_left(lambda: deep_left(kind, c).wait_send())
            at_right(lambda: deep_right(kind, c).wait_send())
        for s in (2, 3):
            at_left(lambda: to_left(s, c).wait_send())
            at_right(lambda: to_right(s, c).wait_send())
        return carry

    lax.fori_loop(0, chunks, finish, 0)
    own_to_sibling(seg).wait_send()
    @pl.when(source)
    def _():
        for i in range(direct):
            to_across(seg, order(x_par, i)).wait_send()

    @pl.when(jnp.logical_not(source))
    def _():
        for i in range(direct):
            to_across(seg, order(1 - y_lo, i)).wait_send()

    @pl.when(early)
    def _():
        for i in shares:
            to_ahead(gathered, order(x_par, i)).wait_send()

    @pl.when(jnp.logical_not(early))
    def _():
        for i in shares:
            to_partner(gathered, order(y_lo, i)).wait_send()

    for q in range(pieces):
        to_sibling(gathered, q).wait_send()
    film_copy(seg, 0, sibling).wait_send()
    film_copy(seg, 1, across).wait_send()
    film_copy(gathered, 2, sibling).wait_send()

    def returned(c, carry):
        back_out(c).wait_send()
        back_in(c).wait_recv()
        return carry

    lax.fori_loop(0, chunks, returned, 0)


def shards(geometry, clips, timesteps, gain, temporal_weight, film_weight, out_weight, skip_weight):
    C, chunks, frames = geometry
    pieces = 4 * C // LANES
    base = np.exp(-math.log(10000.0) * np.arange(C // 2) / (C // 2))
    freq = jnp.asarray(np.concatenate([base, base])[None, :].astype(np.float32))
    hbm = pl.BlockSpec(memory_space=pltpu.HBM)
    bf16, f32 = jnp.bfloat16, jnp.float32
    dma = pltpu.SemaphoreType.DMA
    flops = 2 * 22 * C * C * 2 * chunks * LANES
    return pl.pallas_call(
        functools.partial(unet_kernel, geometry),
        out_shape=pltpu.VMEM(clips.shape, bf16),
        in_specs=[hbm] * 8,
        out_specs=pl.BlockSpec(memory_space=pltpu.VMEM),
        scratch_shapes=[
            pltpu.SMEM(timesteps.shape, jnp.int32),
            pltpu.VMEM(freq.shape, f32),
            pltpu.VMEM(gain.shape, f32),
            pltpu.VMEM((4 * C, C), bf16),
            pltpu.VMEM((2 * C, C), bf16),
            pltpu.VMEM((C, C), bf16),
            pltpu.VMEM((SECTIONS, C, 4 * C), bf16),
            pltpu.VMEM((2, C, C), bf16),
            pltpu.VMEM((SECTIONS, EMB_ROWS, C), f32),
            pltpu.VMEM((SECTIONS, C, LANES), f32),
            pltpu.VMEM((SECTIONS, C, LANES), f32),
            pltpu.VMEM((6, chunks, C, LANES), bf16),
            pltpu.VMEM((6, chunks, C, LANES), bf16),
            pltpu.VMEM((4, C, LANES), bf16),
            pltpu.VMEM((3, 2, chunks, C, LANES), bf16),
            pltpu.VMEM((2, 2, chunks, C, LANES), bf16),
            pltpu.VMEM((2, chunks, C, LANES), bf16),
            pltpu.VMEM((2, chunks, C, LANES), bf16),
            pltpu.VMEM((chunks, C, LANES), bf16),
            dma((10,)),
            dma((chunks,)),
            dma((chunks,)),
            dma((chunks,)),
            dma((2, 2, chunks)),
            dma((2, 2, chunks)),
            dma((2, 2, chunks)),
            dma((2, 2, chunks)),
            dma((1,)),
            dma((1,)),
            dma((pieces,)),
            dma((pieces,)),
            dma((pieces,)),
            dma((pieces,)),
            dma((pieces,)),
            dma((pieces,)),
            dma((3,)),
            dma((3,)),
            dma((chunks,)),
            dma((chunks,)),
        ],
        compiler_params=pltpu.CompilerParams(
            collective_id=0, has_side_effects=True, vmem_limit_bytes=60 * 10**6
        ),
        cost_estimate=pl.CostEstimate(flops=flops, bytes_accessed=4 * clips.size, transcendentals=0),
        name="unet",
    )(timesteps, freq, gain, temporal_weight, film_weight, out_weight, skip_weight, clips)


def solution(mesh):
    frames = mesh.shape["frame"]

    def run(clips, *rest):
        _, _, C, pix = clips.shape
        geometry = (C, pix // 2 // LANES, frames)
        return shards(geometry, clips, *rest)

    placed = (
        P("segment", "frame", None, None),
        P(),
        P(),
        P("segment", None, None, None),
        P("segment", None, None),
        P("segment", None, None),
        P(),
    )
    return jax.shard_map(
        run,
        mesh=mesh,
        in_specs=placed,
        out_specs=P("segment", "frame", None, None),
        check_vma=False,
    )
```
